1024 devices in a mesh: rad: 16 (over z, core), lat: 8 (over x), lon: 8 (over y).
Axes of the slice: x: 8, y: 8, z: 8, core: 2. Of those that a mesh axis runs over, the one named last changes fastest.
Arguments:
- gradient: float32 [64, 128, 1024], P('rad', 'lat', 'lon')
- conductance: float32 [64, 128, 1024], P('rad', 'lat', 'lon'), may hold values from 0.3 to 1
- s_hist: float32 [10, 64, 128, 1024], P(None, 'rad', 'lat', 'lon')
- y_hist: float32 [10, 64, 128, 1024], P(None, 'rad', 'lat', 'lon'), as said below
Outputs:
- smoothed: float32 [64, 128, 1024], P('rad', 'lat', 'lon')
- direction: float32 [64, 128, 1024], P('rad', 'lat', 'lon')
The draws below stay inside these ranges and needn't reach their ends.
Inputs may be any that keep to these rules, and one draw needn't show every extreme that they name: For every pair the sum over all cells of s_hist times y_hist is positive.
All inputs are finite; a program needn't handle non-finite values.
Results may differ from the reference program's by a relative error of at most 0.00021.
Values sent between devices are 32-bit elements; how exact they have to be, the bound alone decides.
A program may use at most 32 MiB of HBM per device.

```python
import math
import jax
import jax.numpy as jnp

PAIRS = 10
STEPS = 12
NRAD = 64
NLAT = 128
NLON = 1024


def history_pairs(key):
    normals = jnp.clip(jax.random.normal(key, (PAIRS, NRAD, NLAT, NLON), jnp.float32), -4.0, 4.0)
    rad_ramp = 1.0 + 2.0 * jnp.arange(NRAD).astype(jnp.float32) / NRAD
    lat_ramp = 1.0 + 2.0 * jnp.arange(NLAT).astype(jnp.float32) / NLAT
    ramp = jnp.sqrt(rad_ramp[:, None, None] * lat_ramp[None, :, None])
    pair_scale = jnp.exp(jax.random.uniform(jax.random.fold_in(key, 11), (PAIRS,), jnp.float32, math.log(0.5), math.log(2.0)))
    return normals * ramp[None] * pair_scale[:, None, None, None]


def draw_s_hist(key, part):
    shared = history_pairs(key)
    return shared


def draw_y_hist(key, part):
    shared = history_pairs(key)
    key = jax.random.fold_in(key, 2)
    first_key, second_key = jax.random.split(key)
    shape = (PAIRS, NRAD, NLAT, NLON)
    curvature = jnp.exp(jax.random.uniform(first_key, shape, jnp.float32, math.log(0.5), math.log(2.0)))
    noise = 0.3 * jnp.clip(jax.random.normal(second_key, shape, jnp.float32), -3.0, 3.0)
    return curvature * shared + noise


def draw_gradient(key, part):
    shared = history_pairs(key)
    key = jax.random.fold_in(key, 3)
    first_key, second_key = jax.random.split(key)
    weights = 0.5 * jnp.clip(jax.random.normal(first_key, (PAIRS,), jnp.float32), -2.0, 2.0)
    total = 0.5 * jnp.clip(jax.random.normal(second_key, (NRAD, NLAT, NLON), jnp.float32), -4.0, 4.0)
    for position in range(PAIRS):
        total = total + weights[position] * shared[position]
    return total


def block_levels(rng, shape, cuts, low, high):
    factor_of = 1.0
    for axis_at, blocks in cuts:
        heights = jax.random.uniform(jax.random.fold_in(jax.random.fold_in(rng, 6), axis_at), (blocks,), jnp.float32, low / len(cuts), high / len(cuts))
        factor_of = factor_of * jnp.repeat(jnp.exp(heights), shape[axis_at] // blocks).reshape((-1,) + (1,) * (len(shape) - 1 - axis_at))
    return factor_of


def setup_inputs(seed: int = 0) -> dict:
    seeds = jax.random.split(jax.random.key(seed), 5)
    gradient = draw_gradient(jax.random.fold_in(seeds[4], 71), 0)
    conductance = jnp.clip(jnp.exp(math.log(1.0) - 1.2039728 * jax.random.uniform(seeds[1], (NRAD, NLAT, NLON), jnp.float32) ** block_levels(seeds[1], (NRAD, NLAT, NLON), ((0, 16), (1, 8), (2, 8)), -0.2, 0.2)), 0.3, 1.0)
    s_hist = draw_s_hist(jax.random.fold_in(seeds[4], 71), 0)
    y_hist = draw_y_hist(jax.random.fold_in(seeds[4], 71), 0)
    return {"gradient": gradient, "conductance": conductance, "s_hist": s_hist, "y_hist": y_hist}


radial_weight = 0.05
latitude_weight = 0.15
longitude_weight = 0.25


def relax(box, kappa):
    center = box[1:-1, 1:-1, 1:-1]
    lap_r = box[2:, 1:-1, 1:-1] + box[:-2, 1:-1, 1:-1] - 2.0 * center
    lap_a = box[1:-1, 2:, 1:-1] + box[1:-1, :-2, 1:-1] - 2.0 * center
    lap_o = box[1:-1, 1:-1, 2:] + box[1:-1, 1:-1, :-2] - 2.0 * center
    return center + kappa * (radial_weight * lap_r + latitude_weight * lap_a + longitude_weight * lap_o)


def extend(field):
    padded = jnp.pad(field, ((1, 1), (1, 1), (0, 0)))
    return jnp.concatenate([padded[:, :, -1:], padded, padded[:, :, :1]], axis=2)


def reference(gradient, conductance, s_hist, y_hist):
    field = gradient
    for number in range(STEPS):
        field = relax(extend(field), conductance)
    smoothed = field
    count = s_hist.shape[0]
    current = smoothed
    alphas = [None] * count
    inverses = [None] * count
    for position in reversed(range(count)):
        inverses[position] = 1.0 / jnp.sum(s_hist[position] * y_hist[position])
        alphas[position] = inverses[position] * jnp.sum(s_hist[position] * current)
        current = current - alphas[position] * y_hist[position]
    scaling = jnp.sum(s_hist[-1] * y_hist[-1]) / jnp.sum(y_hist[-1] * y_hist[-1])
    result = scaling * current
    for position in range(count):
        beta_value = inverses[position] * jnp.sum(y_hist[position] * result)
        result = result + (alphas[position] - beta_value) * s_hist[position]
    return smoothed, -result
```

```python
import functools

import jax
import jax.numpy as jnp
from jax import lax
from jax.experimental import pallas as pl
from jax.experimental.pallas import tpu as pltpu
from jax.sharding import PartitionSpec as P

STEPS = 12
AXES = ("rad", "lat", "lon")
MESH = pl.DeviceIdType.MESH

RAD, LAT, LON = 4, 16, 128
WIDE = 12
GROUP = 16
radial_weight = 0.05
latitude_weight = 0.15
longitude_weight = 0.25
F32 = jnp.float32


def ordered(n):
    return sorted(range(1, n), key=lambda d: -min(d, n - d))


def kernel(sizes, g_hbm, k_hbm, s_hbm, y_hbm, smooth_ref, dir_ref, raw, hist, packs, ua, ka, ub, x2a, x2b, x2c, x3a, x3b, x3c,
           gram_send, gram_recv, b_recv, coef, load_sem, send_sem, recv_sem, gs_sem, gr_sem, bs_sem, br_sem):
    n_rad, n_lat, n_lon = sizes
    pairs = s_hbm.shape[0]
    me = tuple(lax.axis_index(a) for a in AXES)

    def peer(*offset):
        return tuple(lax.rem(m + (o % n), n) if o % n else m for m, o, n in zip(me, offset, sizes))

    started = []

    def send(src, dst, ssem, rsem, target):
        copy = pltpu.make_async_remote_copy(src_ref=src, dst_ref=dst, send_sem=ssem, recv_sem=rsem, device_id=target,
                                            device_id_type=MESH)
        copy.start()
        started.append(copy)
        return copy

    load_g = pltpu.make_async_copy(g_hbm, raw.at[0, pl.ds(RAD, RAD), pl.ds(0, LAT)], load_sem.at[0])
    load_k = pltpu.make_async_copy(k_hbm, raw.at[1, pl.ds(RAD, RAD), pl.ds(0, LAT)], load_sem.at[1])
    load_s = pltpu.make_async_copy(s_hbm, hist.at[0], load_sem.at[2])
    load_y = pltpu.make_async_copy(y_hbm, hist.at[1], load_sem.at[3])
    for copy in (load_g, load_k, load_s, load_y):
        copy.start()

    plane = [(a, o) for a in (-1, 0, 1) for o in (-1, 0, 1) if (a, o) != (0, 0)]
    partners = {(0, a % n_lat, o % n_lon) for a, o in plane}
    partners |= {(d, 0, 0) for d in range(1, n_rad)}
    partners |= {(0, d, 0) for d in range(1, n_lat)}
    partners |= {(0, 0, d) for d in range(1, n_lon)}
    partners = sorted(partners)
    barrier = pltpu.get_barrier_semaphore()
    for offset in partners:
        pl.semaphore_signal(barrier, inc=1, device_id=peer(*offset), device_id_type=MESH)

    lane = lax.broadcasted_iota(jnp.int32, (8, LON), 1)
    sub = lax.broadcasted_iota(jnp.int32, (8, LON), 0)

    load_g.wait()
    load_k.wait()
    to_right = jnp.zeros((2, 8, LON), F32)
    to_left = jnp.zeros((2, 8, LON), F32)
    for spot in range(2 * RAD):
        tile = raw[:, RAD + spot // 2, pl.ds(8 * (spot % 2), 8), :]
        here = (lane // GROUP == spot)[None]
        to_right = jnp.where(here, pltpu.roll(tile, (GROUP * spot + GROUP) % LON, 2), to_right)
        to_left = jnp.where(here, pltpu.roll(tile, GROUP * spot, 2) if spot else tile, to_left)
    packs[1, 1, 0] = to_right
    packs[1, 0, 0] = to_left

    pl.semaphore_wait(barrier, len(partners))

    arrive = []
    order = [(a, o) for a in (-1, 1, 0) for o in (-1, 1)]
    for number, (a, o) in enumerate(order):
        side = 1 if o == 1 else 0
        arrive.append(send(packs.at[1, side, 0], packs.at[1, side, 2 + a], send_sem.at[number], recv_sem.at[number],
                           peer(0, a, o)))
    own = pl.ds(RAD, RAD)
    for number, a, first, to in ((6, -1, 0, LAT), (7, 1, LAT - WIDE, LAT + WIDE)):
        arrive.append(send(raw.at[:, own, pl.ds(first, WIDE)], raw.at[:, own, pl.ds(to, WIDE)], send_sem.at[number],
                           recv_sem.at[number], peer(0, a, 0)))
    ends = ((1, 0), (-1, 2 * RAD))
    faces = []
    for number, (r, to) in enumerate(ends):
        faces.append(send(raw.at[:, own, pl.ds(0, LAT)], raw.at[:, pl.ds(to, RAD), pl.ds(0, LAT)], send_sem.at[8 + number],
                          recv_sem.at[8 + number], peer(r, 0, 0)))

    load_s.wait()
    load_y.wait()
    wide_lane = lane[None]
    total = jnp.zeros((pairs, 8, LON), F32)
    for j in range(pairs):
        acc_s = jnp.zeros((pairs, 8, LON), F32)
        acc_y = jnp.zeros((pairs, 8, LON), F32)
        for spot in range(2 * RAD):
            rows = pl.ds(8 * (spot % 2), 8)
            one = hist[1, j, spot // 2, rows, :][None]
            acc_s += hist[0, :, spot // 2, rows, :] * one
            acc_y += hist[1, :, spot // 2, rows, :] * one
        total = jnp.where(wide_lane == j, jnp.sum(acc_s, axis=2, keepdims=True), total)
        total = jnp.where(wide_lane == GROUP + j, jnp.sum(acc_y, axis=2, keepdims=True), total)
    gram_send[0] = jnp.zeros((16, LON), F32)
    gram_send[0, pl.ds(0, pairs)] = jnp.sum(total, axis=1)

    for copy in arrive[6:]:
        copy.wait_recv()
    ring = pl.ds(LAT, 2 * WIDE)
    for number, (r, to) in enumerate(ends):
        faces.append(send(raw.at[:, own, ring], raw.at[:, pl.ds(to, RAD), ring], send_sem.at[10 + number],
                          recv_sem.at[10 + number], peer(r, 0, 0)))
    for copy in arrive[:6]:
        copy.wait_recv()
    for number, (r, to) in enumerate(ends):
        faces.append(send(packs.at[1, :, pl.ds(1, 3)], packs.at[to // RAD, :, pl.ds(1, 3)], send_sem.at[12 + number],
                          recv_sem.at[12 + number], peer(r, 0, 0)))

    def gram_start(stage):
        n = sizes[stage]
        copies = []
        for d in ordered(n):
            offset = [0, 0, 0]
            offset[stage] = d
            copies.append(send(gram_send.at[stage_slot[stage]], gram_recv.at[stage, d - 1], gs_sem.at[stage, d - 1],
                               gr_sem.at[stage, d - 1], peer(*offset)))
        return copies

    stage_slot = {1: 0, 2: 1, 0: 2}

    def gram_end(stage, copies):
        for copy in copies:
            copy.wait_recv()
        return gram_send[stage_slot[stage]] + jnp.sum(gram_recv[stage, pl.ds(0, sizes[stage] - 1)], axis=0)

    gram_copies = gram_start(1)

    for copy in faces:
        copy.wait_recv()

    low_rad = (me[0] > 0).astype(F32)
    high_rad = (me[0] < n_rad - 1).astype(F32)
    low_lat = (me[1] > 0).astype(F32)
    high_lat = (me[1] < n_lat - 1).astype(F32)
    tile_masks = (1.0, 1.0, high_lat, jnp.where(sub < 4, high_lat, low_lat), low_lat)
    for block, rad_mask in ((0, low_rad), (1, 1.0), (2, high_rad)):
        halo = []
        for slot in (1, 2, 3):
            right, left = packs[block, 0, slot], packs[block, 1, slot]
            tiles = []
            for spot in range(2 * RAD):
                a = pltpu.roll(right, (LON - GROUP * spot) % LON, 2) if spot else right
                b = pltpu.roll(left, LON - GROUP - GROUP * spot, 2) if spot < 7 else left
                tiles.append(jnp.where((lane < LON // 2)[None], a, b))
            halo.append(tiles)
        for layer in range(RAD):
            high, mid, low = (halo[s][2 * layer:2 * layer + 2] for s in (0, 1, 2))
            columns = (mid[0], mid[1], high[0], jnp.where((sub < 4)[None], high[1], low[0]), low[1])
            at = RAD * block + layer
            for t in range(5):
                mask = tile_masks[t] * rad_mask
                rows = pl.ds(8 * t, 8)
                main = raw[:, at, rows, :]
                ua[at, rows, pl.ds(0, LON)] = main[0] * mask
                ua[at, rows, pl.ds(LON, LON)] = columns[t][0] * mask
                ka[at, rows, pl.ds(0, LON)] = main[1] * (mask * radial_weight)
                ka[at, rows, pl.ds(LON, LON)] = columns[t][1] * (mask * radial_weight)

    def advance(src, dst, depth, pick, lo, hi):
        rows = src.shape[1]

        def layer(r):
            value = src[r]
            if lo is not None and r < RAD:
                value = value * lo
            if hi is not None and r >= 2 * RAD:
                value = value * hi
            return value

        before, here = layer(depth - 1), layer(depth)
        for r in range(depth, 3 * RAD - depth):
            after = layer(r + 1)
            lat = pltpu.roll(here, 1, 0) + pltpu.roll(here, rows - 1, 0)
            lon = pltpu.roll(here, 1, 1) + pltpu.roll(here, 2 * LON - 1, 1)
            dst(r, here + pick(r) * ((before + after) + 3.0 * lat + (5.0 * lon - 18.0 * here)))
            before, here = here, after

    def store(ref):
        def put(r, value):
            ref[r] = value
        return put

    def pick1(r):
        return ka[r]

    def pick2(r):
        return jnp.concatenate([ka[r, pl.ds(0, 24)], ka[r, pl.ds(32, 8)]], axis=0)

    wide_sub = lax.broadcasted_iota(jnp.int32, (8, 2 * LON), 0)

    def pick3(r):
        seam = jnp.where(wide_sub < 4, ka[r, pl.ds(16, 8)], ka[r, pl.ds(32, 8)])
        return jnp.concatenate([ka[r, pl.ds(0, 16)], seam], axis=0)

    def keep2(r, value):
        x2a[r, pl.ds(0, 24)] = value[0:24]
        x2a[r, pl.ds(24, 8)] = value[32:40]

    def keep3(r, value):
        x3a[r, pl.ds(0, 16)] = value[0:16]
        x3a[r, pl.ds(16, 8)] = jnp.where(wide_sub < 4, value[16:24], value[24:32])

    def exchange(ref, number):
        return [send(ref.at[own], ref.at[pl.ds(to, RAD)], send_sem.at[number + i], recv_sem.at[number + i], peer(r, 0, 0))
                for i, (r, to) in enumerate(ends)]

    advance(ua, store(ub), 1, pick1, None, None)
    advance(ub, store(ua), 2, pick1, None, None)
    advance(ua, store(ub), 3, pick1, None, None)
    advance(ub, keep2, 4, pick1, None, None)
    copies = exchange(x2a, 14)
    gram_send[1] = gram_end(1, gram_copies)
    gram_copies = gram_start(2)
    for copy in copies:
        copy.wait_recv()
    advance(x2a, store(x2b), 1, pick2, low_rad, high_rad)
    advance(x2b, store(x2c), 2, pick2, None, None)
    advance(x2c, store(x2b), 3, pick2, None, None)
    advance(x2b, keep3, 4, pick2, None, None)
    copies = exchange(x3a, 16)
    gram_send[2] = gram_end(2, gram_copies)
    gram_copies = gram_start(0)
    for copy in copies:
        copy.wait_recv()
    advance(x3a, store(x3b), 1, pick3, low_rad, high_rad)
    advance(x3b, store(x3c), 2, pick3, None, None)
    advance(x3c, store(x3b), 3, pick3, None, None)

    def finish(r, value):
        smooth_ref[r - RAD] = value[0:LAT, 0:LON]

    advance(x3b, finish, 4, pick3, None, None)

    acc = [jnp.zeros((pairs, 8, LON), F32) for _ in range(2)]
    for spot in range(2 * RAD):
        rows = pl.ds(8 * (spot % 2), 8)
        field = smooth_ref[spot // 2, rows, :][None]
        acc = [acc[h] + hist[h, :, spot // 2, rows, :] * field for h in range(2)]
    line = jnp.zeros((8, LON), F32)
    for h in range(2):
        sums = jnp.sum(acc[h], axis=2, keepdims=True)
        for i in range(pairs):
            line = jnp.where(lane == GROUP * h + i, sums[i], line)

    def add_up(stage, row):
        b_recv[stage, pl.ds(0, 1)] = row
        copies = []
        for d in ordered(sizes[stage]):
            offset = [0, 0, 0]
            offset[stage] = d
            copies.append(send(b_recv.at[stage, pl.ds(0, 1)], b_recv.at[stage, pl.ds(d, 1)], bs_sem.at[stage, d - 1],
                               br_sem.at[stage, d - 1], peer(*offset)))
        return copies

    def added(stage, copies):
        for copy in copies:
            copy.wait_recv()
        return jnp.sum(b_recv[stage, pl.ds(0, sizes[stage])], axis=0, keepdims=True)

    copies = add_up(1, jnp.sum(line, axis=0, keepdims=True))

    gram = gram_end(0, gram_copies)
    col = lax.broadcasted_iota(jnp.int32, (16, LON), 1)
    row = lax.broadcasted_iota(jnp.int32, (16, LON), 0)
    inside = row < pairs
    diagonal = (col == row) & inside
    d = jnp.sum(jnp.where(diagonal, gram, 0.0), axis=1, keepdims=True)
    inverse = 1.0 / jnp.where(inside[:, 0:1], d, 1.0)
    scaling = gram[pairs - 1:pairs, pairs - 1:pairs] / gram[pairs - 1:pairs, GROUP + pairs - 1:GROUP + pairs]
    upper = jnp.where((col > row) & (col < pairs), gram * inverse, 0.0)
    solve = jnp.where(diagonal, 1.0, 0.0)
    for k in range(pairs - 1, 0, -1):
        solve = solve - upper[:, k:k + 1] * solve[k:k + 1, :]
    inverse_row = jnp.sum(jnp.where(diagonal, inverse, 0.0), axis=0, keepdims=True)
    alpha = solve * inverse_row
    right = d * alpha
    for k in range(pairs):
        right = right + (scaling * gram[:, GROUP + k:GROUP + k + 1]) * alpha[k:k + 1, :]
    right = jnp.where((col == row + GROUP) & inside, -scaling, right)
    for k in range(pairs - 1):
        column = jnp.sum(jnp.where(col == row, upper[k:k + 1, :], 0.0), axis=1, keepdims=True)
        right = right - column * right[k:k + 1, :]
    of_s = -(right * inverse)
    of_y = scaling * alpha

    copies = add_up(2, added(1, copies))
    copies = add_up(0, added(2, copies))
    b = added(0, copies)
    coef[0] = jnp.broadcast_to(jnp.sum(of_s * b, axis=1, keepdims=True), (16, LON))
    coef[1] = jnp.broadcast_to(jnp.sum(of_y * b, axis=1, keepdims=True), (16, LON))
    for spot in range(2 * RAD):
        rows = pl.ds(8 * (spot % 2), 8)
        value = -scaling * smooth_ref[spot // 2, rows, :]
        for i in range(pairs):
            value = value + coef[0, pl.ds(i, 1)] * hist[0, i, spot // 2, rows, :]
            value = value + coef[1, pl.ds(i, 1)] * hist[1, i, spot // 2, rows, :]
        dir_ref[spot // 2, rows, :] = value

    for copy in started:
        copy.wait_send()


def per_device(sizes, gradient, conductance, s_hist, y_hist):
    pairs = s_hist.shape[0]
    most = max(sizes)
    vmem, dma = pltpu.VMEM, pltpu.SemaphoreType.DMA
    shape = jax.ShapeDtypeStruct(gradient.shape, F32)
    return pl.pallas_call(
        functools.partial(kernel, sizes),
        out_shape=(shape, shape),
        in_specs=[pl.BlockSpec(memory_space=pltpu.HBM)] * 4,
        out_specs=(pl.BlockSpec(memory_space=vmem),) * 2,
        scratch_shapes=[
            vmem((2, 3 * RAD, 40, LON), F32),
            vmem((2, pairs, RAD, LAT, LON), F32),
            vmem((3, 2, 4, 2, 8, LON), F32),
            vmem((3 * RAD, 40, 2 * LON), F32),
            vmem((3 * RAD, 40, 2 * LON), F32),
            vmem((3 * RAD, 40, 2 * LON), F32),
            vmem((3 * RAD, 32, 2 * LON), F32),
            vmem((3 * RAD, 32, 2 * LON), F32),
            vmem((3 * RAD, 32, 2 * LON), F32),
            vmem((3 * RAD, 24, 2 * LON), F32),
            vmem((3 * RAD, 24, 2 * LON), F32),
            vmem((3 * RAD, 24, 2 * LON), F32),
            vmem((3, 16, LON), F32),
            vmem((3, most - 1, 16, LON), F32),
            vmem((3, 16, LON), F32),
            vmem((2, 16, LON), F32),
            dma((4,)),
            dma((18,)),
            dma((18,)),
            dma((3, most - 1)),
            dma((3, most - 1)),
            dma((3, most - 1)),
            dma((3, most - 1)),
        ],
        compiler_params=pltpu.CompilerParams(collective_id=0, has_side_effects=True, vmem_limit_bytes=60 * 2**20),
        cost_estimate=pl.CostEstimate(flops=20_000_000, bytes_accessed=800_000, transcendentals=0),
        name="filter_and_direction",
    )(gradient, conductance, s_hist, y_hist)


def solution(mesh):
    sizes = tuple(mesh.shape[a] for a in AXES)
    field, history = P(*AXES), P(None, *AXES)
    return jax.shard_map(
        functools.partial(per_device, sizes),
        mesh=mesh,
        in_specs=(field, field, history, history),
        out_specs=(field, field),
        check_vma=False,
    )
```

```python
import functools

import jax
import jax.numpy as jnp
from jax import lax
from jax.experimental import pallas as pl
from jax.experimental.pallas import tpu as pltpu
from jax.sharding import PartitionSpec as P

STEPS = 12
AXES = ("rad", "lat", "lon")
MESH = pl.DeviceIdType.MESH

RAD, LAT, LON = 4, 16, 128
WIDE = 12
GROUP = 16
radial_weight = 0.05
latitude_weight = 0.15
longitude_weight = 0.25
F32 = jnp.float32


def ordered(n):
    return sorted(range(1, n), key=lambda d: -min(d, n - d))


def kernel(sizes, g_hbm, k_hbm, s_hbm, y_hbm, smooth_ref, dir_ref, raw, hist, edges, packs, ua, ka, ub, x2a, x2b, x2c, x3a,
           x3b, x3c, gram_send, gram_recv, plane_row, rad_row, coef, load_sem, halo_sent, halo_here, face_sent, face_here,
           gram_sent, gram_here, row_sent, row_here, near_in, far_in):
    n_rad, n_lat, n_lon = sizes
    pairs = s_hbm.shape[0]
    me = tuple(lax.axis_index(a) for a in AXES)

    def peer(*offset):
        return tuple(lax.rem(m + (o % n), n) if o % n else m for m, o, n in zip(me, offset, sizes))

    owed = []

    def send(src, dst, ssem, rsem, target):
        pltpu.make_async_remote_copy(src_ref=src, dst_ref=dst, send_sem=ssem, recv_sem=rsem, device_id=target,
                                     device_id_type=MESH).start()

    def wait_bytes(ref, sem):
        pltpu.make_async_copy(ref, ref, sem).wait()

    load_g = pltpu.make_async_copy(g_hbm, raw.at[0, pl.ds(RAD, RAD), pl.ds(0, LAT)], load_sem.at[0])
    load_k = pltpu.make_async_copy(k_hbm, raw.at[1, pl.ds(RAD, RAD), pl.ds(0, LAT)], load_sem.at[1])
    load_s = pltpu.make_async_copy(s_hbm, hist.at[0], load_sem.at[2])
    load_y = pltpu.make_async_copy(y_hbm, hist.at[1], load_sem.at[3])
    for copy in (load_g, load_k, load_s, load_y):
        copy.start()

    near = (0, -1, 1)
    cube = [(r, a, o) for r in near for a in near for o in near][1:]
    cube.sort(key=lambda c: -sum(map(abs, c)))
    barrier = pltpu.get_barrier_semaphore()
    for offset in cube:
        pl.semaphore_signal(barrier, inc=1, device_id=peer(*offset), device_id_type=MESH)

    lane = lax.broadcasted_iota(jnp.int32, (8, LON), 1)
    sub = lax.broadcasted_iota(jnp.int32, (8, LON), 0)

    load_g.wait()
    load_k.wait()
    to_right = jnp.zeros((2, 8, LON), F32)
    to_left = jnp.zeros((2, 8, LON), F32)
    for spot in range(2 * RAD):
        tile = raw[:, RAD + spot // 2, pl.ds(8 * (spot % 2), 8), :]
        here = (lane // GROUP == spot)[None]
        to_right = jnp.where(here, pltpu.roll(tile, (GROUP * spot + GROUP) % LON, 2), to_right)
        to_left = jnp.where(here, pltpu.roll(tile, GROUP * spot, 2) if spot else tile, to_left)
    edges[0] = to_left
    edges[1] = to_right

    pl.semaphore_wait(barrier, len(cube))

    own = pl.ds(RAD, RAD)

    def block_of(r):
        return 1 - r

    rows_of = {-1: (0, WIDE, LAT), 0: (0, LAT, 0), 1: (LAT - WIDE, WIDE, LAT + WIDE)}

    def halo(r, a, o):
        at = block_of(r)
        if o:
            side = (o + 1) // 2
            send(edges.at[side], packs.at[at, side, 1 + a], halo_sent.at[3], halo_here.at[3], peer(r, a, o))
        else:
            first, count, to = rows_of[a]
            send(raw.at[:, own, pl.ds(first, count)], raw.at[:, pl.ds(RAD * at, RAD), pl.ds(to, count)], halo_sent.at[at],
                 halo_here.at[at], peer(r, a, o))

    for offset in cube:
        halo(*offset)
    halos = ((raw.at[:, pl.ds(0, RAD)], 0), (raw.at[:, own, pl.ds(LAT, 2 * WIDE)], 1), (raw.at[:, pl.ds(2 * RAD, RAD)], 2),
             (packs, 3))
    owed += [(ref, halo_sent.at[number]) for ref, number in halos]

    load_s.wait()
    load_y.wait()
    total = [jnp.zeros((8, LON), F32) for _ in range(-(-pairs // 4))]
    for j in range(pairs):
        acc_s = jnp.zeros((pairs, 8, LON), F32)
        acc_y = jnp.zeros((pairs, 8, LON), F32)
        for spot in range(2 * RAD):
            rows = pl.ds(8 * (spot % 2), 8)
            one = hist[1, j, spot // 2, rows, :][None]
            acc_s += hist[0, :, spot // 2, rows, :] * one
            acc_y += hist[1, :, spot // 2, rows, :] * one
        sum_s = jnp.sum(acc_s, axis=2, keepdims=True)
        sum_y = jnp.sum(acc_y, axis=2, keepdims=True)
        for i in range(pairs):
            at = 32 * (i % 4) + j
            total[i // 4] = jnp.where(lane == at, sum_s[i], jnp.where(lane == at + GROUP, sum_y[i], total[i // 4]))
    for line, value in enumerate(total):
        gram_send[0, pl.ds(line, 1)] = jnp.sum(value, axis=0, keepdims=True)
    lines = pl.ds(0, len(total))

    for ref, number in halos:
        wait_bytes(ref, halo_here.at[number])

    signs = (0, -2, 2)
    outer = [(0, a, o) for a in signs for o in signs][1:] + [(-2, 0, 0), (2, 0, 0)]
    for offset in outer:
        pl.semaphore_signal(near_in, inc=1, device_id=peer(*offset), device_id_type=MESH)

    turn = {1: 0, 2: 1, 0: 2}

    def gram_start(stage):
        at = turn[stage]
        for d in ordered(sizes[stage]):
            offset = [0, 0, 0]
            offset[stage] = d
            send(gram_send.at[at, lines], gram_recv.at[at, d - 1, lines], gram_sent.at[at], gram_here.at[at], peer(*offset))
        owed.append((gram_recv.at[at, pl.ds(0, sizes[stage] - 1), lines], gram_sent.at[at]))

    def gram_end(stage):
        at = turn[stage]
        ref = gram_recv.at[at, pl.ds(0, sizes[stage] - 1), lines]
        wait_bytes(ref, gram_here.at[at])
        return gram_send[at, lines] + jnp.sum(gram_recv[at, pl.ds(0, sizes[stage] - 1), lines], axis=0)

    low_rad = (me[0] > 0).astype(F32)
    high_rad = (me[0] < n_rad - 1).astype(F32)
    low_lat = (me[1] > 0).astype(F32)
    high_lat = (me[1] < n_lat - 1).astype(F32)
    tile_masks = (1.0, 1.0, high_lat, jnp.where(sub < 4, high_lat, low_lat), low_lat)
    for block, rad_mask in ((0, low_rad), (1, 1.0), (2, high_rad)):
        sides = []
        for slot in range(3):
            right, left = packs[block, 0, slot], packs[block, 1, slot]
            tiles = []
            for spot in range(2 * RAD):
                a = pltpu.roll(right, (LON - GROUP * spot) % LON, 2) if spot else right
                b = pltpu.roll(left, LON - GROUP - GROUP * spot, 2) if spot < 7 else left
                tiles.append(jnp.where((lane < LON // 2)[None], a, b))
            sides.append(tiles)
        for layer in range(RAD):
            high, mid, low = (sides[s][2 * layer:2 * layer + 2] for s in (0, 1, 2))
            columns = (mid[0], mid[1], high[0], jnp.where((sub < 4)[None], high[1], low[0]), low[1])
            at = RAD * block + layer
            for t in range(5):
                mask = tile_masks[t] * rad_mask
                rows = pl.ds(8 * t, 8)
                main = raw[:, at, rows, :]
                ua[at, rows, pl.ds(0, LON)] = main[0] * mask
                ua[at, rows, pl.ds(LON, LON)] = columns[t][0] * mask
                ka[at, rows, pl.ds(0, LON)] = main[1] * (mask * radial_weight)
                ka[at, rows, pl.ds(LON, LON)] = columns[t][1] * (mask * radial_weight)

    def advance(src, dst, depth, pick, lo, hi):
        rows = src.shape[1]

        def layer(r):
            value = src[r]
            if lo is not None and r < RAD:
                value = value * lo
            if hi is not None and r >= 2 * RAD:
                value = value * hi
            return value

        before, here = layer(depth - 1), layer(depth)
        for r in range(depth, 3 * RAD - depth):
            after = layer(r + 1)
            lat = pltpu.roll(here, 1, 0) + pltpu.roll(here, rows - 1, 0)
            lon = pltpu.roll(here, 1, 1) + pltpu.roll(here, 2 * LON - 1, 1)
            dst(r, here + pick(r) * ((before + after) + 3.0 * lat + (5.0 * lon - 18.0 * here)))
            before, here = here, after

    def store(ref):
        def put(r, value):
            ref[r] = value
        return put

    def pick1(r):
        return ka[r]

    def pick2(r):
        return jnp.concatenate([ka[r, pl.ds(0, 24)], ka[r, pl.ds(32, 8)]], axis=0)

    wide_sub = lax.broadcasted_iota(jnp.int32, (8, 2 * LON), 0)

    def pick3(r):
        seam = jnp.where(wide_sub < 4, ka[r, pl.ds(16, 8)], ka[r, pl.ds(32, 8)])
        return jnp.concatenate([ka[r, pl.ds(0, 16)], seam], axis=0)

    def keep2(r, value):
        x2a[r, pl.ds(0, 24)] = value[0:24]
        x2a[r, pl.ds(24, 8)] = value[32:40]

    def keep3(r, value):
        x3a[r, pl.ds(0, 16)] = value[0:16]
        x3a[r, pl.ds(16, 8)] = jnp.where(wide_sub < 4, value[16:24], value[24:32])

    def exchange(ref, number):
        for r in (1, -1):
            send(ref.at[own], ref.at[pl.ds(RAD * block_of(r), RAD)], face_sent.at[number], face_here.at[number], peer(r, 0, 0))
        owed.append((ref.at[pl.ds(0, 2 * RAD)], face_sent.at[number]))

    def exchanged(ref, number):
        wait_bytes(ref.at[pl.ds(0, 2 * RAD)], face_here.at[number])

    advance(ua, store(ub), 1, pick1, None, None)
    advance(ub, store(ua), 2, pick1, None, None)
    advance(ua, store(ub), 3, pick1, None, None)
    advance(ub, keep2, 4, pick1, None, None)
    exchange(x2a, 0)
    pl.semaphore_wait(near_in, len(outer))
    for r in (-4, 4):
        pl.semaphore_signal(far_in, inc=1, device_id=peer(r, 0, 0), device_id_type=MESH)
    gram_start(1)
    exchanged(x2a, 0)
    advance(x2a, store(x2b), 1, pick2, low_rad, high_rad)
    advance(x2b, store(x2c), 2, pick2, None, None)
    advance(x2c, store(x2b), 3, pick2, None, None)
    advance(x2b, keep3, 4, pick2, None, None)
    exchange(x3a, 1)
    pl.semaphore_wait(far_in, 2)
    exchanged(x3a, 1)
    gram_send[1, lines] = gram_end(1)
    gram_start(2)
    advance(x3a, store(x3b), 1, pick3, low_rad, high_rad)
    advance(x3b, store(x3c), 2, pick3, None, None)
    advance(x3c, store(x3b), 3, pick3, None, None)

    def finish(r, value):
        smooth_ref[r - RAD] = value[0:LAT, 0:LON]

    advance(x3b, finish, 4, pick3, None, None)

    acc = [jnp.zeros((pairs, 8, LON), F32) for _ in range(2)]
    for spot in range(2 * RAD):
        rows = pl.ds(8 * (spot % 2), 8)
        field = smooth_ref[spot // 2, rows, :][None]
        acc = [acc[h] + hist[h, :, spot // 2, rows, :] * field for h in range(2)]
    line = jnp.zeros((8, LON), F32)
    for h in range(2):
        sums = jnp.sum(acc[h], axis=2, keepdims=True)
        for i in range(pairs):
            line = jnp.where(lane == GROUP * h + i, sums[i], line)

    def hops(offset):
        return sum(min(d, n - d) for d, n in zip(offset, sizes))

    def add_up(buf, row, offsets, number):
        count = len(offsets)
        buf[pl.ds(count, 1)] = row
        for at, offset in enumerate(sorted(offsets, key=lambda c: -hops(c))):
            send(buf.at[pl.ds(count, 1)], buf.at[pl.ds(at, 1)], row_sent.at[number], row_here.at[number], peer(*offset))
        owed.append((buf.at[pl.ds(0, count)], row_sent.at[number]))

    def added(buf, offsets, number):
        count = len(offsets)
        wait_bytes(buf.at[pl.ds(0, count)], row_here.at[number])
        return jnp.sum(buf[pl.ds(0, count + 1)], axis=0, keepdims=True)

    in_plane = [(0, a, o) for a in range(n_lat) for o in range(n_lon)][1:]
    in_rad = [(r, 0, 0) for r in range(1, n_rad)]
    add_up(plane_row, jnp.sum(line, axis=0, keepdims=True), in_plane, 0)
    gram_send[2, lines] = gram_end(2)
    gram_start(0)
    add_up(rad_row, added(plane_row, in_plane, 0), in_rad, 1)

    packed = gram_end(0)
    parts = [pltpu.roll(packed[i // 4:i // 4 + 1], LON - 32 * (i % 4), 1) if i % 4 else packed[i // 4:i // 4 + 1]
             for i in range(pairs)]
    gram = jnp.concatenate(parts + [jnp.zeros((16 - pairs, LON), F32)], axis=0)
    col = lax.broadcasted_iota(jnp.int32, (16, LON), 1)
    row = lax.broadcasted_iota(jnp.int32, (16, LON), 0)
    inside = row < pairs
    diagonal = (col == row) & inside
    d = jnp.sum(jnp.where(diagonal, gram, 0.0), axis=1, keepdims=True)
    inverse = 1.0 / jnp.where(inside[:, 0:1], d, 1.0)
    scaling = gram[pairs - 1:pairs, pairs - 1:pairs] / gram[pairs - 1:pairs, GROUP + pairs - 1:GROUP + pairs]
    upper = jnp.where((col > row) & (col < pairs), gram * inverse, 0.0)
    solve = jnp.where(diagonal, 1.0, 0.0)
    for k in range(pairs - 1, 0, -1):
        solve = solve - upper[:, k:k + 1] * solve[k:k + 1, :]
    inverse_row = jnp.sum(jnp.where(diagonal, inverse, 0.0), axis=0, keepdims=True)
    alpha = solve * inverse_row
    right = d * alpha
    for k in range(pairs):
        right = right + (scaling * gram[:, GROUP + k:GROUP + k + 1]) * alpha[k:k + 1, :]
    right = jnp.where((col == row + GROUP) & inside, -scaling, right)
    for k in range(pairs - 1):
        column = jnp.sum(jnp.where(col == row, upper[k:k + 1, :], 0.0), axis=1, keepdims=True)
        right = right - column * right[k:k + 1, :]
    of_s = -(right * inverse)
    of_y = scaling * alpha

    b = added(rad_row, in_rad, 1)
    coef[0] = jnp.broadcast_to(jnp.sum(of_s * b, axis=1, keepdims=True), (16, LON))
    coef[1] = jnp.broadcast_to(jnp.sum(of_y * b, axis=1, keepdims=True), (16, LON))
    for spot in range(2 * RAD):
        rows = pl.ds(8 * (spot % 2), 8)
        value = -scaling * smooth_ref[spot // 2, rows, :]
        for i in range(pairs):
            value = value + coef[0, pl.ds(i, 1)] * hist[0, i, spot // 2, rows, :]
            value = value + coef[1, pl.ds(i, 1)] * hist[1, i, spot // 2, rows, :]
        dir_ref[spot // 2, rows, :] = value

    for ref, sem in owed:
        wait_bytes(ref, sem)


def per_device(sizes, gradient, conductance, s_hist, y_hist):
    pairs = s_hist.shape[0]
    most = max(sizes)
    vmem, dma = pltpu.VMEM, pltpu.SemaphoreType.DMA
    shape = jax.ShapeDtypeStruct(gradient.shape, F32)
    return pl.pallas_call(
        functools.partial(kernel, sizes),
        out_shape=(shape, shape),
        in_specs=[pl.BlockSpec(memory_space=pltpu.HBM)] * 4,
        out_specs=(pl.BlockSpec(memory_space=vmem),) * 2,
        scratch_shapes=[
            vmem((2, 3 * RAD, 40, LON), F32),
            vmem((2, pairs, RAD, LAT, LON), F32),
            vmem((2, 2, 8, LON), F32),
            vmem((3, 2, 3, 2, 8, LON), F32),
            vmem((3 * RAD, 40, 2 * LON), F32),
            vmem((3 * RAD, 40, 2 * LON), F32),
            vmem((3 * RAD, 40, 2 * LON), F32),
            vmem((3 * RAD, 32, 2 * LON), F32),
            vmem((3 * RAD, 32, 2 * LON), F32),
            vmem((3 * RAD, 32, 2 * LON), F32),
            vmem((3 * RAD, 24, 2 * LON), F32),
            vmem((3 * RAD, 24, 2 * LON), F32),
            vmem((3 * RAD, 24, 2 * LON), F32),
            vmem((3, 8, LON), F32),
            vmem((3, most - 1, 8, LON), F32),
            vmem((sizes[1] * sizes[2], LON), F32),
            vmem((sizes[0], LON), F32),
            vmem((2, 16, LON), F32),
            dma((4,)),
            dma((4,)),
            dma((4,)),
            dma((2,)),
            dma((2,)),
            dma((3,)),
            dma((3,)),
            dma((2,)),
            dma((2,)),
            pltpu.SemaphoreType.REGULAR,
            pltpu.SemaphoreType.REGULAR,
        ],
        compiler_params=pltpu.CompilerParams(collective_id=0, has_side_effects=True, vmem_limit_bytes=60 * 2**20),
        cost_estimate=pl.CostEstimate(flops=20_000_000, bytes_accessed=800_000, transcendentals=0),
        name="filter_and_direction",
    )(gradient, conductance, s_hist, y_hist)


def solution(mesh):
    sizes = tuple(mesh.shape[a] for a in AXES)
    field, history = P(*AXES), P(None, *AXES)
    return jax.shard_map(
        functools.partial(per_device, sizes),
        mesh=mesh,
        in_specs=(field, field, history, history),
        out_specs=(field, field),
        check_vma=False,
    )
```

```python
import functools

import jax
import jax.numpy as jnp
from jax import lax
from jax.experimental import pallas as pl
from jax.experimental.pallas import tpu as pltpu
from jax.sharding import PartitionSpec as P

STEPS = 12
AXES = ("rad", "lat", "lon")
MESH = pl.DeviceIdType.MESH

RAD, LAT, LON = 4, 16, 128
WIDE = 12
GROUP = 16
radial_weight = 0.05
latitude_weight = 0.15
longitude_weight = 0.25
F32 = jnp.float32


def ordered(n):
    return sorted(range(1, n), key=lambda d: -min(d, n - d))


def kernel(sizes, g_hbm, k_hbm, s_hbm, y_hbm, out_ref, raw, hist, edges, packs, ua, ka, ub, x2a, x2b, x2c, x3a,
           x3b, x3c, gram_send, gram_recv, plane_row, rad_row, coef, load_sem, halo_sent, halo_here, face_sent, face_here,
           gram_sent, gram_here, row_sent, row_here, near_in, far_in):
    n_rad, n_lat, n_lon = sizes
    pairs = s_hbm.shape[0]
    minus_smooth, minus_dir = out_ref.at[0], out_ref.at[1]
    me = tuple(lax.axis_index(a) for a in AXES)

    def peer(*offset):
        return tuple(lax.rem(m + (o % n), n) if o % n else m for m, o, n in zip(me, offset, sizes))

    owed = []

    def send(src, dst, ssem, rsem, target):
        pltpu.make_async_remote_copy(src_ref=src, dst_ref=dst, send_sem=ssem, recv_sem=rsem, device_id=target,
                                     device_id_type=MESH).start()

    def wait_bytes(ref, sem):
        pltpu.make_async_copy(ref, ref, sem).wait()

    load_g = pltpu.make_async_copy(g_hbm, raw.at[0, pl.ds(RAD, RAD), pl.ds(0, LAT)], load_sem.at[0])
    load_k = pltpu.make_async_copy(k_hbm, raw.at[1, pl.ds(RAD, RAD), pl.ds(0, LAT)], load_sem.at[1])
    load_s = pltpu.make_async_copy(s_hbm, hist.at[0], load_sem.at[2])
    load_y = pltpu.make_async_copy(y_hbm, hist.at[1], load_sem.at[3])
    for copy in (load_g, load_k, load_s, load_y):
        copy.start()

    near = (0, -1, 1)
    cube = [(r, a, o) for r in near for a in near for o in near][1:]
    cube.sort(key=lambda c: -sum(map(abs, c)))
    barrier = pltpu.get_barrier_semaphore()
    for offset in cube:
        pl.semaphore_signal(barrier, inc=1, device_id=peer(*offset), device_id_type=MESH)

    lane = lax.broadcasted_iota(jnp.int32, (8, LON), 1)
    sub = lax.broadcasted_iota(jnp.int32, (8, LON), 0)

    load_g.wait()
    load_k.wait()
    to_right = jnp.zeros((2, 8, LON), F32)
    to_left = jnp.zeros((2, 8, LON), F32)
    for spot in range(2 * RAD):
        tile = raw[:, RAD + spot // 2, pl.ds(8 * (spot % 2), 8), :]
        here = (lane // GROUP == spot)[None]
        to_right = jnp.where(here, pltpu.roll(tile, (GROUP * spot + GROUP) % LON, 2), to_right)
        to_left = jnp.where(here, pltpu.roll(tile, GROUP * spot, 2) if spot else tile, to_left)
    edges[0] = to_left
    edges[1] = to_right

    pl.semaphore_wait(barrier, len(cube))

    own = pl.ds(RAD, RAD)

    def block_of(r):
        return 1 - r

    rows_of = {-1: (0, WIDE, LAT), 0: (0, LAT, 0), 1: (LAT - WIDE, WIDE, LAT + WIDE)}

    def halo(r, a, o):
        at = block_of(r)
        if o:
            side = (o + 1) // 2
            send(edges.at[side], packs.at[at, side, 1 + a], halo_sent.at[3], halo_here.at[3], peer(r, a, o))
        else:
            first, count, to = rows_of[a]
            send(raw.at[:, own, pl.ds(first, count)], raw.at[:, pl.ds(RAD * at, RAD), pl.ds(to, count)], halo_sent.at[at],
                 halo_here.at[at], peer(r, a, o))

    for offset in cube:
        halo(*offset)
    halos = ((raw.at[:, pl.ds(0, RAD)], 0), (raw.at[:, own, pl.ds(LAT, 2 * WIDE)], 1), (raw.at[:, pl.ds(2 * RAD, RAD)], 2),
             (packs, 3))
    owed += [(ref, halo_sent.at[number]) for ref, number in halos]

    load_s.wait()
    load_y.wait()
    total = [jnp.zeros((8, LON), F32) for _ in range(-(-pairs // 4))]
    for j in range(pairs):
        acc_s = jnp.zeros((pairs, 8, LON), F32)
        acc_y = jnp.zeros((pairs, 8, LON), F32)
        for spot in range(2 * RAD):
            rows = pl.ds(8 * (spot % 2), 8)
            one = hist[1, j, spot // 2, rows, :][None]
            acc_s += hist[0, :, spot // 2, rows, :] * one
            acc_y += hist[1, :, spot // 2, rows, :] * one
        sum_s = jnp.sum(acc_s, axis=2, keepdims=True)
        sum_y = jnp.sum(acc_y, axis=2, keepdims=True)
        for i in range(pairs):
            at = 32 * (i % 4) + j
            total[i // 4] = jnp.where(lane == at, sum_s[i], jnp.where(lane == at + GROUP, sum_y[i], total[i // 4]))
    for line, value in enumerate(total):
        gram_send[0, pl.ds(line, 1)] = jnp.sum(value, axis=0, keepdims=True)
    lines = pl.ds(0, len(total))

    for ref, number in halos:
        wait_bytes(ref, halo_here.at[number])

    signs = (0, -2, 2)
    outer = [(0, a, o) for a in signs for o in signs][1:] + [(-2, 0, 0), (2, 0, 0)]
    for offset in outer:
        pl.semaphore_signal(near_in, inc=1, device_id=peer(*offset), device_id_type=MESH)

    turn = {1: 0, 2: 1, 0: 2}

    def gram_start(stage):
        at = turn[stage]
        for d in ordered(sizes[stage]):
            offset = [0, 0, 0]
            offset[stage] = d
            send(gram_send.at[at, lines], gram_recv.at[at, d - 1, lines], gram_sent.at[at], gram_here.at[at], peer(*offset))
        owed.append((gram_recv.at[at, pl.ds(0, sizes[stage] - 1), lines], gram_sent.at[at]))

    def gram_end(stage):
        at = turn[stage]
        ref = gram_recv.at[at, pl.ds(0, sizes[stage] - 1), lines]
        wait_bytes(ref, gram_here.at[at])
        return gram_send[at, lines] + jnp.sum(gram_recv[at, pl.ds(0, sizes[stage] - 1), lines], axis=0)

    low_rad = (me[0] > 0).astype(F32)
    high_rad = (me[0] < n_rad - 1).astype(F32)
    low_lat = (me[1] > 0).astype(F32)
    high_lat = (me[1] < n_lat - 1).astype(F32)
    tile_masks = (1.0, 1.0, high_lat, jnp.where(sub < 4, high_lat, low_lat), low_lat)
    for block, rad_mask in ((0, low_rad), (1, 1.0), (2, high_rad)):
        sides = []
        for slot in range(3):
            right, left = packs[block, 0, slot], packs[block, 1, slot]
            tiles = []
            for spot in range(2 * RAD):
                a = pltpu.roll(right, (LON - GROUP * spot) % LON, 2) if spot else right
                b = pltpu.roll(left, LON - GROUP - GROUP * spot, 2) if spot < 7 else left
                tiles.append(jnp.where((lane < LON // 2)[None], a, b))
            sides.append(tiles)
        for layer in range(RAD):
            high, mid, low = (sides[s][2 * layer:2 * layer + 2] for s in (0, 1, 2))
            columns = (mid[0], mid[1], high[0], jnp.where((sub < 4)[None], high[1], low[0]), low[1])
            at = RAD * block + layer
            for t in range(5):
                mask = tile_masks[t] * rad_mask
                rows = pl.ds(8 * t, 8)
                main = raw[:, at, rows, :]
                ua[at, rows, pl.ds(0, LON)] = main[0] * mask
                ua[at, rows, pl.ds(LON, LON)] = columns[t][0] * mask
                ka[at, rows, pl.ds(0, LON)] = main[1] * (mask * radial_weight)
                ka[at, rows, pl.ds(LON, LON)] = columns[t][1] * (mask * radial_weight)

    def advance(src, dst, depth, pick, lo, hi):
        rows = src.shape[1]

        def layer(r):
            value = src[r]
            if lo is not None and r < RAD:
                value = value * lo
            if hi is not None and r >= 2 * RAD:
                value = value * hi
            return value

        before, here = layer(depth - 1), layer(depth)
        for r in range(depth, 3 * RAD - depth):
            after = layer(r + 1)
            lat = pltpu.roll(here, 1, 0) + pltpu.roll(here, rows - 1, 0)
            lon = pltpu.roll(here, 1, 1) + pltpu.roll(here, 2 * LON - 1, 1)
            dst(r, here + pick(r) * ((before + after) + 3.0 * lat + (5.0 * lon - 18.0 * here)))
            before, here = here, after

    def store(ref):
        def put(r, value):
            ref[r] = value
        return put

    def pick1(r):
        return ka[r]

    def pick2(r):
        return jnp.concatenate([ka[r, pl.ds(0, 24)], ka[r, pl.ds(32, 8)]], axis=0)

    wide_sub = lax.broadcasted_iota(jnp.int32, (8, 2 * LON), 0)

    def pick3(r):
        seam = jnp.where(wide_sub < 4, ka[r, pl.ds(16, 8)], ka[r, pl.ds(32, 8)])
        return jnp.concatenate([ka[r, pl.ds(0, 16)], seam], axis=0)

    def keep2(r, value):
        x2a[r, pl.ds(0, 24)] = value[0:24]
        x2a[r, pl.ds(24, 8)] = value[32:40]

    def keep3(r, value):
        x3a[r, pl.ds(0, 16)] = value[0:16]
        x3a[r, pl.ds(16, 8)] = jnp.where(wide_sub < 4, value[16:24], value[24:32])

    def exchange(ref, number):
        for r in (1, -1):
            send(ref.at[own], ref.at[pl.ds(RAD * block_of(r), RAD)], face_sent.at[number], face_here.at[number], peer(r, 0, 0))
        owed.append((ref.at[pl.ds(0, 2 * RAD)], face_sent.at[number]))

    def exchanged(ref, number):
        wait_bytes(ref.at[pl.ds(0, 2 * RAD)], face_here.at[number])

    advance(ua, store(ub), 1, pick1, None, None)
    advance(ub, store(ua), 2, pick1, None, None)
    advance(ua, store(ub), 3, pick1, None, None)
    advance(ub, keep2, 4, pick1, None, None)
    exchange(x2a, 0)
    pl.semaphore_wait(near_in, len(outer))
    for r in (-4, 4):
        pl.semaphore_signal(far_in, inc=1, device_id=peer(r, 0, 0), device_id_type=MESH)
    gram_start(1)
    exchanged(x2a, 0)
    advance(x2a, store(x2b), 1, pick2, low_rad, high_rad)
    advance(x2b, store(x2c), 2, pick2, None, None)
    advance(x2c, store(x2b), 3, pick2, None, None)
    advance(x2b, keep3, 4, pick2, None, None)
    exchange(x3a, 1)
    pl.semaphore_wait(far_in, 2)
    exchanged(x3a, 1)
    gram_send[1, lines] = gram_end(1)
    gram_start(2)
    advance(x3a, store(x3b), 1, pick3, low_rad, high_rad)
    advance(x3b, store(x3c), 2, pick3, None, None)
    advance(x3c, store(x3b), 3, pick3, None, None)

    def finish(r, value):
        minus_smooth[r - RAD] = -value[0:LAT, 0:LON]

    advance(x3b, finish, 4, pick3, None, None)

    acc = [jnp.zeros((pairs, 8, LON), F32) for _ in range(2)]
    for spot in range(2 * RAD):
        rows = pl.ds(8 * (spot % 2), 8)
        field = -minus_smooth[spot // 2, rows, :][None]
        acc = [acc[h] + hist[h, :, spot // 2, rows, :] * field for h in range(2)]
    line = jnp.zeros((8, LON), F32)
    for h in range(2):
        sums = jnp.sum(acc[h], axis=2, keepdims=True)
        for i in range(pairs):
            line = jnp.where(lane == GROUP * h + i, sums[i], line)

    def hops(offset):
        return sum(min(d, n - d) for d, n in zip(offset, sizes))

    def add_up(buf, row, offsets, number):
        count = len(offsets)
        buf[pl.ds(count, 1)] = row
        for at, offset in enumerate(sorted(offsets, key=lambda c: -hops(c))):
            send(buf.at[pl.ds(count, 1)], buf.at[pl.ds(at, 1)], row_sent.at[number], row_here.at[number], peer(*offset))
        owed.append((buf.at[pl.ds(0, count)], row_sent.at[number]))

    def added(buf, offsets, number):
        count = len(offsets)
        wait_bytes(buf.at[pl.ds(0, count)], row_here.at[number])
        return jnp.sum(buf[pl.ds(0, count + 1)], axis=0, keepdims=True)

    in_plane = [(0, a, o) for a in range(n_lat) for o in range(n_lon)][1:]
    in_rad = [(r, 0, 0) for r in range(1, n_rad)]
    add_up(plane_row, jnp.sum(line, axis=0, keepdims=True), in_plane, 0)
    gram_send[2, lines] = gram_end(2)
    gram_start(0)
    add_up(rad_row, added(plane_row, in_plane, 0), in_rad, 1)

    packed = gram_end(0)
    parts = [pltpu.roll(packed[i // 4:i // 4 + 1], LON - 32 * (i % 4), 1) if i % 4 else packed[i // 4:i // 4 + 1]
             for i in range(pairs)]
    gram = jnp.concatenate(parts + [jnp.zeros((16 - pairs, LON), F32)], axis=0)
    col = lax.broadcasted_iota(jnp.int32, (16, LON), 1)
    row = lax.broadcasted_iota(jnp.int32, (16, LON), 0)
    inside = row < pairs
    diagonal = (col == row) & inside
    d = jnp.sum(jnp.where(diagonal, gram, 0.0), axis=1, keepdims=True)
    inverse = 1.0 / jnp.where(inside[:, 0:1], d, 1.0)
    scaling = gram[pairs - 1:pairs, pairs - 1:pairs] / gram[pairs - 1:pairs, GROUP + pairs - 1:GROUP + pairs]
    upper = jnp.where((col > row) & (col < pairs), gram * inverse, 0.0)
    solve = jnp.where(diagonal, 1.0, 0.0)
    for k in range(pairs - 1, 0, -1):
        solve = solve - upper[:, k:k + 1] * solve[k:k + 1, :]
    inverse_row = jnp.sum(jnp.where(diagonal, inverse, 0.0), axis=0, keepdims=True)
    alpha = solve * inverse_row
    right = d * alpha
    for k in range(pairs):
        right = right + (scaling * gram[:, GROUP + k:GROUP + k + 1]) * alpha[k:k + 1, :]
    right = jnp.where((col == row + GROUP) & inside, -scaling, right)
    for k in range(pairs - 1):
        column = jnp.sum(jnp.where(col == row, upper[k:k + 1, :], 0.0), axis=1, keepdims=True)
        right = right - column * right[k:k + 1, :]
    of_s = right * inverse
    of_y = -scaling * alpha

    b = added(rad_row, in_rad, 1)
    coef[0] = jnp.broadcast_to(jnp.sum(of_s * b, axis=1, keepdims=True), (16, LON))
    coef[1] = jnp.broadcast_to(jnp.sum(of_y * b, axis=1, keepdims=True), (16, LON))
    for spot in range(2 * RAD):
        rows = pl.ds(8 * (spot % 2), 8)
        value = -scaling * minus_smooth[spot // 2, rows, :]
        for i in range(pairs):
            value = value + coef[0, pl.ds(i, 1)] * hist[0, i, spot // 2, rows, :]
            value = value + coef[1, pl.ds(i, 1)] * hist[1, i, spot // 2, rows, :]
        minus_dir[spot // 2, rows, :] = value

    for ref, sem in owed:
        wait_bytes(ref, sem)


def per_device(sizes, gradient, conductance, s_hist, y_hist):
    pairs = s_hist.shape[0]
    most = max(sizes)
    vmem, dma = pltpu.VMEM, pltpu.SemaphoreType.DMA
    inputs = [pltpu.with_memory_space_constraint(a, pltpu.HBM) for a in (gradient, conductance, s_hist, y_hist)]
    out = pl.pallas_call(
        functools.partial(kernel, sizes),
        out_shape=pltpu.VMEM((2,) + gradient.shape, F32),
        in_specs=[pl.BlockSpec(memory_space=pltpu.HBM)] * 4,
        out_specs=pl.BlockSpec(memory_space=vmem),
        scratch_shapes=[
            vmem((2, 3 * RAD, 40, LON), F32),
            vmem((2, pairs, RAD, LAT, LON), F32),
            vmem((2, 2, 8, LON), F32),
            vmem((3, 2, 3, 2, 8, LON), F32),
            vmem((3 * RAD, 40, 2 * LON), F32),
            vmem((3 * RAD, 40, 2 * LON), F32),
            vmem((3 * RAD, 40, 2 * LON), F32),
            vmem((3 * RAD, 32, 2 * LON), F32),
            vmem((3 * RAD, 32, 2 * LON), F32),
            vmem((3 * RAD, 32, 2 * LON), F32),
            vmem((3 * RAD, 24, 2 * LON), F32),
            vmem((3 * RAD, 24, 2 * LON), F32),
            vmem((3 * RAD, 24, 2 * LON), F32),
            vmem((3, 8, LON), F32),
            vmem((3, most - 1, 8, LON), F32),
            vmem((sizes[1] * sizes[2], LON), F32),
            vmem((sizes[0], LON), F32),
            vmem((2, 16, LON), F32),
            dma((4,)),
            dma((4,)),
            dma((4,)),
            dma((2,)),
            dma((2,)),
            dma((3,)),
            dma((3,)),
            dma((2,)),
            dma((2,)),
            pltpu.SemaphoreType.REGULAR,
            pltpu.SemaphoreType.REGULAR,
        ],
        compiler_params=pltpu.CompilerParams(collective_id=0, has_side_effects=True, vmem_limit_bytes=24 * 2**20),
        cost_estimate=pl.CostEstimate(flops=20_000_000, bytes_accessed=800_000, transcendentals=0),
        name="filter_and_direction",
    )(*inputs)
    return -out[0], -out[1]


def solution(mesh):
    sizes = tuple(mesh.shape[a] for a in AXES)
    field, history = P(*AXES), P(None, *AXES)
    return jax.shard_map(
        functools.partial(per_device, sizes),
        mesh=mesh,
        in_specs=(field, field, history, history),
        out_specs=(field, field),
        check_vma=False,
    )
```

```python
import functools

import jax
import jax.numpy as jnp
from jax import lax
from jax.experimental import pallas as pl
from jax.experimental.pallas import tpu as pltpu
from jax.sharding import PartitionSpec as P

STEPS = 12
AXES = ("rad", "lat", "lon")
MESH = pl.DeviceIdType.MESH

RAD, LAT, LON = 4, 16, 128
WIDE = 12
GROUP = 16
radial_weight = 0.05
latitude_weight = 0.15
longitude_weight = 0.25
F32 = jnp.float32


def ordered(n):
    return sorted(range(1, n), key=lambda d: -min(d, n - d))


def kernel(sizes, g_hbm, k_hbm, s_hbm, y_hbm, out_ref, raw, hist, edges, packs, ua, ka, ub, x2a, x2b, x2c, x3a,
           x3b, x3c, side2, side3, gram_send, gram_recv, plane_row, rad_row, coef, load_sem, halo_sent, halo_here, face_sent, face_here,
           gram_sent, gram_here, row_sent, row_here, near_in, far_in):
    n_rad, n_lat, n_lon = sizes
    pairs = s_hbm.shape[0]
    minus_smooth, minus_dir = out_ref.at[0], out_ref.at[1]
    me = tuple(lax.axis_index(a) for a in AXES)

    def peer(*offset):
        return tuple(lax.rem(m + (o % n), n) if o % n else m for m, o, n in zip(me, offset, sizes))

    owed = []

    def send(src, dst, ssem, rsem, target):
        pltpu.make_async_remote_copy(src_ref=src, dst_ref=dst, send_sem=ssem, recv_sem=rsem, device_id=target,
                                     device_id_type=MESH).start()

    def wait_bytes(ref, sem):
        pltpu.make_async_copy(ref, ref, sem).wait()

    load_g = pltpu.make_async_copy(g_hbm, raw.at[0, pl.ds(RAD, RAD), pl.ds(0, LAT)], load_sem.at[0])
    load_k = pltpu.make_async_copy(k_hbm, raw.at[1, pl.ds(RAD, RAD), pl.ds(0, LAT)], load_sem.at[1])
    load_s = pltpu.make_async_copy(s_hbm, hist.at[0], load_sem.at[2])
    load_y = pltpu.make_async_copy(y_hbm, hist.at[1], load_sem.at[3])
    for copy in (load_g, load_k, load_s, load_y):
        copy.start()

    near = (0, -1, 1)
    cube = [(r, a, o) for r in near for a in near for o in near][1:]
    cube.sort(key=lambda c: -sum(map(abs, c)))
    barrier = pltpu.get_barrier_semaphore()
    for offset in cube:
        pl.semaphore_signal(barrier, inc=1, device_id=peer(*offset), device_id_type=MESH)

    lane = lax.broadcasted_iota(jnp.int32, (8, LON), 1)
    sub = lax.broadcasted_iota(jnp.int32, (8, LON), 0)

    load_g.wait()
    load_k.wait()
    to_right = jnp.zeros((2, 8, LON), F32)
    to_left = jnp.zeros((2, 8, LON), F32)
    for spot in range(2 * RAD):
        tile = raw[:, RAD + spot // 2, pl.ds(8 * (spot % 2), 8), :]
        here = (lane // GROUP == spot)[None]
        to_right = jnp.where(here, pltpu.roll(tile, (GROUP * spot + GROUP) % LON, 2), to_right)
        to_left = jnp.where(here, pltpu.roll(tile, GROUP * spot, 2) if spot else tile, to_left)
    edges[0] = to_left
    edges[1] = to_right

    pl.semaphore_wait(barrier, len(cube))

    own = pl.ds(RAD, RAD)

    def block_of(r):
        return 1 - r

    rows_of = {-1: (0, WIDE, LAT), 0: (0, LAT, 0), 1: (LAT - WIDE, WIDE, LAT + WIDE)}

    def halo(r, a, o):
        at = block_of(r)
        if o:
            side = (o + 1) // 2
            send(edges.at[side], packs.at[at, side, 1 + a], halo_sent.at[3], halo_here.at[3], peer(r, a, o))
        else:
            first, count, to = rows_of[a]
            send(raw.at[:, own, pl.ds(first, count)], raw.at[:, pl.ds(RAD * at, RAD), pl.ds(to, count)], halo_sent.at[at],
                 halo_here.at[at], peer(r, a, o))

    for offset in cube:
        halo(*offset)
    halos = ((raw.at[:, pl.ds(0, RAD)], 0), (raw.at[:, own, pl.ds(LAT, 2 * WIDE)], 1), (raw.at[:, pl.ds(2 * RAD, RAD)], 2),
             (packs, 3))
    owed += [(ref, halo_sent.at[number]) for ref, number in halos]

    load_s.wait()
    load_y.wait()
    total = [jnp.zeros((8, LON), F32) for _ in range(-(-pairs // 4))]
    for j in range(pairs):
        acc_s = jnp.zeros((pairs, 8, LON), F32)
        acc_y = jnp.zeros((pairs, 8, LON), F32)
        for spot in range(2 * RAD):
            rows = pl.ds(8 * (spot % 2), 8)
            one = hist[1, j, spot // 2, rows, :][None]
            acc_s += hist[0, :, spot // 2, rows, :] * one
            acc_y += hist[1, :, spot // 2, rows, :] * one
        sum_s = jnp.sum(acc_s, axis=2, keepdims=True)
        sum_y = jnp.sum(acc_y, axis=2, keepdims=True)
        for i in range(pairs):
            at = 32 * (i % 4) + j
            total[i // 4] = jnp.where(lane == at, sum_s[i], jnp.where(lane == at + GROUP, sum_y[i], total[i // 4]))
    for line, value in enumerate(total):
        gram_send[0, pl.ds(line, 1)] = jnp.sum(value, axis=0, keepdims=True)
    lines = pl.ds(0, len(total))

    for ref, number in halos:
        wait_bytes(ref, halo_here.at[number])

    signs = (0, -2, 2)
    outer = [(0, a, o) for a in signs for o in signs][1:] + [(-2, 0, 0), (2, 0, 0)]
    for offset in outer:
        pl.semaphore_signal(near_in, inc=1, device_id=peer(*offset), device_id_type=MESH)

    turn = {1: 0, 2: 1, 0: 2}

    def gram_start(stage):
        at = turn[stage]
        for d in ordered(sizes[stage]):
            offset = [0, 0, 0]
            offset[stage] = d
            send(gram_send.at[at, lines], gram_recv.at[at, d - 1, lines], gram_sent.at[at], gram_here.at[at], peer(*offset))
        owed.append((gram_recv.at[at, pl.ds(0, sizes[stage] - 1), lines], gram_sent.at[at]))

    def gram_end(stage):
        at = turn[stage]
        ref = gram_recv.at[at, pl.ds(0, sizes[stage] - 1), lines]
        wait_bytes(ref, gram_here.at[at])
        return gram_send[at, lines] + jnp.sum(gram_recv[at, pl.ds(0, sizes[stage] - 1), lines], axis=0)

    low_rad = (me[0] > 0).astype(F32)
    high_rad = (me[0] < n_rad - 1).astype(F32)
    low_lat = (me[1] > 0).astype(F32)
    high_lat = (me[1] < n_lat - 1).astype(F32)
    tile_masks = (1.0, 1.0, high_lat, jnp.where(sub < 4, high_lat, low_lat), low_lat)
    for block, rad_mask in ((0, low_rad), (1, 1.0), (2, high_rad)):
        sides = []
        for slot in range(3):
            right, left = packs[block, 0, slot], packs[block, 1, slot]
            tiles = []
            for spot in range(2 * RAD):
                a = pltpu.roll(right, (LON - GROUP * spot) % LON, 2) if spot else right
                b = pltpu.roll(left, LON - GROUP - GROUP * spot, 2) if spot < 7 else left
                tiles.append(jnp.where((lane < LON // 2)[None], a, b))
            sides.append(tiles)
        for layer in range(RAD):
            high, mid, low = (sides[s][2 * layer:2 * layer + 2] for s in (0, 1, 2))
            columns = (mid[0], mid[1], high[0], jnp.where((sub < 4)[None], high[1], low[0]), low[1])
            at = RAD * block + layer
            for t in range(5):
                mask = tile_masks[t] * rad_mask
                rows = pl.ds(8 * t, 8)
                main = raw[:, at, rows, :]
                ua[at, rows, pl.ds(0, LON)] = main[0] * mask
                ua[at, rows, pl.ds(LON, LON)] = columns[t][0] * mask
                ka[at, rows, pl.ds(0, LON)] = main[1] * (mask * radial_weight)
                ka[at, rows, pl.ds(LON, LON)] = columns[t][1] * (mask * radial_weight)

    def advance(src, dst, depth, pick, lo, hi, sides=None):
        rows = src.shape[1]

        def layer(r):
            if sides is not None and not RAD <= r < 2 * RAD:
                packed = sides[1 if r < RAD else 2]
                turn_by = (LON - 32 * (r % RAD)) % LON
                value = jnp.concatenate([src[r, :, pl.ds(0, LON)], pltpu.roll(packed, turn_by, 1) if turn_by else packed], axis=1)
            else:
                value = src[r]
            if lo is not None and r < RAD:
                value = value * lo
            if hi is not None and r >= 2 * RAD:
                value = value * hi
            return value

        before, here = layer(depth - 1), layer(depth)
        for r in range(depth, 3 * RAD - depth):
            after = layer(r + 1)
            lat = pltpu.roll(here, 1, 0) + pltpu.roll(here, rows - 1, 0)
            lon = pltpu.roll(here, 1, 1) + pltpu.roll(here, 2 * LON - 1, 1)
            dst(r, here + pick(r) * ((before + after) + 3.0 * lat + (5.0 * lon - 18.0 * here)))
            before, here = here, after

    def store(ref):
        def put(r, value):
            ref[r] = value
        return put

    def pick1(r):
        return ka[r]

    def pick2(r):
        return jnp.concatenate([ka[r, pl.ds(0, 24)], ka[r, pl.ds(32, 8)]], axis=0)

    wide_sub = lax.broadcasted_iota(jnp.int32, (8, 2 * LON), 0)

    def pick3(r):
        seam = jnp.where(wide_sub < 4, ka[r, pl.ds(16, 8)], ka[r, pl.ds(32, 8)])
        return jnp.concatenate([ka[r, pl.ds(0, 16)], seam], axis=0)

    def keep2(r, value):
        x2a[r, pl.ds(0, 24)] = value[0:24]
        x2a[r, pl.ds(24, 8)] = value[32:40]

    def keep3(r, value):
        x3a[r, pl.ds(0, 16)] = value[0:16]
        x3a[r, pl.ds(16, 8)] = jnp.where(wide_sub < 4, value[16:24], value[24:32])

    def exchange(ref, side, number):
        main = pl.ds(0, LON)
        for r in (1, -1):
            send(ref.at[own, :, main], ref.at[pl.ds(RAD * block_of(r), RAD), :, main], face_sent.at[number, 0],
                 face_here.at[number, 0], peer(r, 0, 0))
        group = (lax.broadcasted_iota(jnp.int32, side.shape[1:], 1) + GROUP) // 32
        packed = ref[RAD, :, pl.ds(LON, LON)]
        for l in range(1, RAD):
            packed = jnp.where(group == l, pltpu.roll(ref[RAD + l, :, pl.ds(LON, LON)], 32 * l, 1), packed)
        side[0] = packed
        for r in (1, -1):
            send(side.at[0], side.at[1 + block_of(r) // 2], face_sent.at[number, 1], face_here.at[number, 1], peer(r, 0, 0))
        owed.append((ref.at[pl.ds(0, 2 * RAD), :, main], face_sent.at[number, 0]))
        owed.append((side.at[pl.ds(1, 2)], face_sent.at[number, 1]))

    def exchanged(ref, side, number):
        wait_bytes(ref.at[pl.ds(0, 2 * RAD), :, pl.ds(0, LON)], face_here.at[number, 0])
        wait_bytes(side.at[pl.ds(1, 2)], face_here.at[number, 1])

    advance(ua, store(ub), 1, pick1, None, None)
    advance(ub, store(ua), 2, pick1, None, None)
    advance(ua, store(ub), 3, pick1, None, None)
    advance(ub, keep2, 4, pick1, None, None)
    exchange(x2a, side2, 0)
    pl.semaphore_wait(near_in, len(outer))
    for r in (-4, 4):
        pl.semaphore_signal(far_in, inc=1, device_id=peer(r, 0, 0), device_id_type=MESH)
    gram_start(1)
    exchanged(x2a, side2, 0)
    advance(x2a, store(x2b), 1, pick2, low_rad, high_rad, side2)
    advance(x2b, store(x2c), 2, pick2, None, None)
    advance(x2c, store(x2b), 3, pick2, None, None)
    advance(x2b, keep3, 4, pick2, None, None)
    exchange(x3a, side3, 1)
    pl.semaphore_wait(far_in, 2)
    gram_send[1, lines] = gram_end(1)
    gram_start(2)
    exchanged(x3a, side3, 1)
    advance(x3a, store(x3b), 1, pick3, low_rad, high_rad, side3)
    advance(x3b, store(x3c), 2, pick3, None, None)
    advance(x3c, store(x3b), 3, pick3, None, None)

    def finish(r, value):
        minus_smooth[r - RAD] = -value[0:LAT, 0:LON]

    advance(x3b, finish, 4, pick3, None, None)

    acc = [jnp.zeros((pairs, 8, LON), F32) for _ in range(2)]
    for spot in range(2 * RAD):
        rows = pl.ds(8 * (spot % 2), 8)
        field = -minus_smooth[spot // 2, rows, :][None]
        acc = [acc[h] + hist[h, :, spot // 2, rows, :] * field for h in range(2)]
    line = jnp.zeros((8, LON), F32)
    for h in range(2):
        sums = jnp.sum(acc[h], axis=2, keepdims=True)
        for i in range(pairs):
            line = jnp.where(lane == GROUP * h + i, sums[i], line)

    def hops(offset):
        return sum(min(d, n - d) for d, n in zip(offset, sizes))

    def add_up(buf, row, offsets, number):
        count = len(offsets)
        buf[pl.ds(count, 1)] = row
        for at, offset in enumerate(sorted(offsets, key=lambda c: -hops(c))):
            send(buf.at[pl.ds(count, 1)], buf.at[pl.ds(at, 1)], row_sent.at[number], row_here.at[number], peer(*offset))
        owed.append((buf.at[pl.ds(0, count)], row_sent.at[number]))

    def added(buf, offsets, number):
        count = len(offsets)
        wait_bytes(buf.at[pl.ds(0, count)], row_here.at[number])
        return jnp.sum(buf[pl.ds(0, count + 1)], axis=0, keepdims=True)

    in_plane = [(0, a, o) for a in range(n_lat) for o in range(n_lon)][1:]
    in_rad = [(r, 0, 0) for r in range(1, n_rad)]
    add_up(plane_row, jnp.sum(line, axis=0, keepdims=True), in_plane, 0)
    gram_send[2, lines] = gram_end(2)
    gram_start(0)
    add_up(rad_row, added(plane_row, in_plane, 0), in_rad, 1)

    packed = gram_end(0)
    parts = [pltpu.roll(packed[i // 4:i // 4 + 1], LON - 32 * (i % 4), 1) if i % 4 else packed[i // 4:i // 4 + 1]
             for i in range(pairs)]
    gram = jnp.concatenate(parts + [jnp.zeros((16 - pairs, LON), F32)], axis=0)
    col = lax.broadcasted_iota(jnp.int32, (16, LON), 1)
    row = lax.broadcasted_iota(jnp.int32, (16, LON), 0)
    inside = row < pairs
    diagonal = (col == row) & inside
    d = jnp.sum(jnp.where(diagonal, gram, 0.0), axis=1, keepdims=True)
    inverse = 1.0 / jnp.where(inside[:, 0:1], d, 1.0)
    scaling = gram[pairs - 1:pairs, pairs - 1:pairs] / gram[pairs - 1:pairs, GROUP + pairs - 1:GROUP + pairs]
    upper = jnp.where((col > row) & (col < pairs), gram * inverse, 0.0)
    solve = jnp.where(diagonal, 1.0, 0.0)
    for k in range(pairs - 1, 0, -1):
        solve = solve - upper[:, k:k + 1] * solve[k:k + 1, :]
    inverse_row = jnp.sum(jnp.where(diagonal, inverse, 0.0), axis=0, keepdims=True)
    alpha = solve * inverse_row
    right = d * alpha
    for k in range(pairs):
        right = right + (scaling * gram[:, GROUP + k:GROUP + k + 1]) * alpha[k:k + 1, :]
    right = jnp.where((col == row + GROUP) & inside, -scaling, right)
    for k in range(pairs - 1):
        column = jnp.sum(jnp.where(col == row, upper[k:k + 1, :], 0.0), axis=1, keepdims=True)
        right = right - column * right[k:k + 1, :]
    of_s = right * inverse
    of_y = -scaling * alpha

    b = added(rad_row, in_rad, 1)
    coef[0] = jnp.broadcast_to(jnp.sum(of_s * b, axis=1, keepdims=True), (16, LON))
    coef[1] = jnp.broadcast_to(jnp.sum(of_y * b, axis=1, keepdims=True), (16, LON))
    for spot in range(2 * RAD):
        rows = pl.ds(8 * (spot % 2), 8)
        value = -scaling * minus_smooth[spot // 2, rows, :]
        for i in range(pairs):
            value = value + coef[0, pl.ds(i, 1)] * hist[0, i, spot // 2, rows, :]
            value = value + coef[1, pl.ds(i, 1)] * hist[1, i, spot // 2, rows, :]
        minus_dir[spot // 2, rows, :] = value

    for ref, sem in owed:
        wait_bytes(ref, sem)


def per_device(sizes, gradient, conductance, s_hist, y_hist):
    pairs = s_hist.shape[0]
    most = max(sizes)
    vmem, dma = pltpu.VMEM, pltpu.SemaphoreType.DMA
    inputs = [pltpu.with_memory_space_constraint(a, pltpu.HBM) for a in (gradient, conductance, s_hist, y_hist)]
    out = pl.pallas_call(
        functools.partial(kernel, sizes),
        out_shape=pltpu.VMEM((2,) + gradient.shape, F32),
        in_specs=[pl.BlockSpec(memory_space=pltpu.HBM)] * 4,
        out_specs=pl.BlockSpec(memory_space=vmem),
        scratch_shapes=[
            vmem((2, 3 * RAD, 40, LON), F32),
            vmem((2, pairs, RAD, LAT, LON), F32),
            vmem((2, 2, 8, LON), F32),
            vmem((3, 2, 3, 2, 8, LON), F32),
            vmem((3 * RAD, 40, 2 * LON), F32),
            vmem((3 * RAD, 40, 2 * LON), F32),
            vmem((3 * RAD, 40, 2 * LON), F32),
            vmem((3 * RAD, 32, 2 * LON), F32),
            vmem((3 * RAD, 32, 2 * LON), F32),
            vmem((3 * RAD, 32, 2 * LON), F32),
            vmem((3 * RAD, 24, 2 * LON), F32),
            vmem((3 * RAD, 24, 2 * LON), F32),
            vmem((3 * RAD, 24, 2 * LON), F32),
            vmem((3, 32, LON), F32),
            vmem((3, 24, LON), F32),
            vmem((3, 8, LON), F32),
            vmem((3, most - 1, 8, LON), F32),
            vmem((sizes[1] * sizes[2], LON), F32),
            vmem((sizes[0], LON), F32),
            vmem((2, 16, LON), F32),
            dma((4,)),
            dma((4,)),
            dma((4,)),
            dma((2, 2)),
            dma((2, 2)),
            dma((3,)),
            dma((3,)),
            dma((2,)),
            dma((2,)),
            pltpu.SemaphoreType.REGULAR,
            pltpu.SemaphoreType.REGULAR,
        ],
        compiler_params=pltpu.CompilerParams(collective_id=0, has_side_effects=True, vmem_limit_bytes=24 * 2**20),
        cost_estimate=pl.CostEstimate(flops=20_000_000, bytes_accessed=800_000, transcendentals=0),
        name="filter_and_direction",
    )(*inputs)
    return -out[0], -out[1]


def solution(mesh):
    sizes = tuple(mesh.shape[a] for a in AXES)
    field, history = P(*AXES), P(None, *AXES)
    return jax.shard_map(
        functools.partial(per_device, sizes),
        mesh=mesh,
        in_specs=(field, field, history, history),
        out_specs=(field, field),
        check_vma=False,
    )
```

```python
import functools

import jax
import jax.numpy as jnp
from jax import lax
from jax.experimental import pallas as pl
from jax.experimental.pallas import tpu as pltpu
from jax.sharding import PartitionSpec as P

STEPS = 12
AXES = ("rad", "lat", "lon")
MESH = pl.DeviceIdType.MESH

RAD, LAT, LON = 4, 16, 128
WIDE = 12
GROUP = 16
radial_weight = 0.05
latitude_weight = 0.15
longitude_weight = 0.25
F32 = jnp.float32


def ordered(n):
    return sorted(range(1, n), key=lambda d: -min(d, n - d))


def kernel(sizes, g_hbm, k_hbm, s_hbm, y_hbm, out_ref, raw, hist, edges, packs, ua, ka, ub, x2a, x2b, x2c, x3a,
           x3b, x3c, side2, side3, va, vb, near_hist, gram_send, gram_recv, plane_row, rad_row, coef, load_sem, halo_sent, halo_here, face_sent, face_here,
           gram_sent, gram_here, row_sent, row_here, hist_sent, hist_here, near_in, far_in):
    n_rad, n_lat, n_lon = sizes
    pairs = s_hbm.shape[0]
    minus_smooth, minus_dir = out_ref.at[0], out_ref.at[1]
    me = tuple(lax.axis_index(a) for a in AXES)

    def peer(*offset):
        return tuple(lax.rem(m + (o % n), n) if o % n else m for m, o, n in zip(me, offset, sizes))

    owed = []

    def send(src, dst, ssem, rsem, target):
        pltpu.make_async_remote_copy(src_ref=src, dst_ref=dst, send_sem=ssem, recv_sem=rsem, device_id=target,
                                     device_id_type=MESH).start()

    def wait_bytes(ref, sem):
        pltpu.make_async_copy(ref, ref, sem).wait()

    load_g = pltpu.make_async_copy(g_hbm, raw.at[0, pl.ds(RAD, RAD), pl.ds(0, LAT)], load_sem.at[0])
    load_k = pltpu.make_async_copy(k_hbm, raw.at[1, pl.ds(RAD, RAD), pl.ds(0, LAT)], load_sem.at[1])
    load_s = pltpu.make_async_copy(s_hbm, hist.at[0], load_sem.at[2])
    load_y = pltpu.make_async_copy(y_hbm, hist.at[1], load_sem.at[3])
    for copy in (load_g, load_k, load_s, load_y):
        copy.start()

    near = (0, -1, 1)
    cube = [(r, a, o) for r in near for a in near for o in near][1:]
    cube.sort(key=lambda c: -sum(map(abs, c)))
    barrier = pltpu.get_barrier_semaphore()
    for offset in cube:
        pl.semaphore_signal(barrier, inc=1, device_id=peer(*offset), device_id_type=MESH)

    lane = lax.broadcasted_iota(jnp.int32, (8, LON), 1)
    sub = lax.broadcasted_iota(jnp.int32, (8, LON), 0)

    load_g.wait()
    load_k.wait()
    to_right = jnp.zeros((2, 8, LON), F32)
    to_left = jnp.zeros((2, 8, LON), F32)
    for spot in range(2 * RAD):
        tile = raw[:, RAD + spot // 2, pl.ds(8 * (spot % 2), 8), :]
        here = (lane // GROUP == spot)[None]
        to_right = jnp.where(here, pltpu.roll(tile, (GROUP * spot + GROUP) % LON, 2), to_right)
        to_left = jnp.where(here, pltpu.roll(tile, GROUP * spot, 2) if spot else tile, to_left)
    edges[0] = to_left
    edges[1] = to_right

    pl.semaphore_wait(barrier, len(cube))

    own = pl.ds(RAD, RAD)

    def block_of(r):
        return 1 - r

    rows_of = {-1: (0, WIDE, LAT), 0: (0, LAT, 0), 1: (LAT - WIDE, WIDE, LAT + WIDE)}

    def halo(r, a, o):
        at = block_of(r)
        if o:
            side = (o + 1) // 2
            send(edges.at[side], packs.at[at, side, 1 + a], halo_sent.at[3], halo_here.at[3], peer(r, a, o))
        else:
            first, count, to = rows_of[a]
            send(raw.at[:, own, pl.ds(first, count)], raw.at[:, pl.ds(RAD * at, RAD), pl.ds(to, count)], halo_sent.at[at],
                 halo_here.at[at], peer(r, a, o))

    for offset in cube:
        halo(*offset)
    halos = ((raw.at[:, pl.ds(0, RAD)], 0), (raw.at[:, own, pl.ds(LAT, 2 * WIDE)], 1), (raw.at[:, pl.ds(2 * RAD, RAD)], 2),
             (packs, 3))
    owed += [(ref, halo_sent.at[number]) for ref, number in halos]

    load_s.wait()
    load_y.wait()
    for r in (1, -1):
        send(hist, near_hist.at[block_of(r) // 2], hist_sent, hist_here, peer(r, 0, 0))
    owed.append((near_hist, hist_sent))

    total = [jnp.zeros((8, LON), F32) for _ in range(-(-pairs // 4))]
    for j in range(pairs):
        acc_s = jnp.zeros((pairs, 8, LON), F32)
        acc_y = jnp.zeros((pairs, 8, LON), F32)
        for spot in range(2 * RAD):
            rows = pl.ds(8 * (spot % 2), 8)
            one = hist[1, j, spot // 2, rows, :][None]
            acc_s += hist[0, :, spot // 2, rows, :] * one
            acc_y += hist[1, :, spot // 2, rows, :] * one
        sum_s = jnp.sum(acc_s, axis=2, keepdims=True)
        sum_y = jnp.sum(acc_y, axis=2, keepdims=True)
        for i in range(pairs):
            at = 32 * (i % 4) + j
            total[i // 4] = jnp.where(lane == at, sum_s[i], jnp.where(lane == at + GROUP, sum_y[i], total[i // 4]))
    for line, value in enumerate(total):
        gram_send[0, pl.ds(line, 1)] = jnp.sum(value, axis=0, keepdims=True)
    lines = pl.ds(0, len(total))

    for ref, number in halos:
        wait_bytes(ref, halo_here.at[number])

    signs = (0, -2, 2)
    outer = [(0, a, o) for a in signs for o in signs][1:] + [(-2, 0, 0), (2, 0, 0)]
    for offset in outer:
        pl.semaphore_signal(near_in, inc=1, device_id=peer(*offset), device_id_type=MESH)

    turn = {1: 0, 2: 1, 0: 2}

    def gram_start(stage):
        at = turn[stage]
        for d in ordered(sizes[stage]):
            offset = [0, 0, 0]
            offset[stage] = d
            send(gram_send.at[at, lines], gram_recv.at[at, d - 1, lines], gram_sent.at[at], gram_here.at[at], peer(*offset))
        owed.append((gram_recv.at[at, pl.ds(0, sizes[stage] - 1), lines], gram_sent.at[at]))

    def gram_end(stage):
        at = turn[stage]
        ref = gram_recv.at[at, pl.ds(0, sizes[stage] - 1), lines]
        wait_bytes(ref, gram_here.at[at])
        return gram_send[at, lines] + jnp.sum(gram_recv[at, pl.ds(0, sizes[stage] - 1), lines], axis=0)

    low_rad = (me[0] > 0).astype(F32)
    high_rad = (me[0] < n_rad - 1).astype(F32)
    low_lat = (me[1] > 0).astype(F32)
    high_lat = (me[1] < n_lat - 1).astype(F32)
    tile_masks = (1.0, 1.0, high_lat, jnp.where(sub < 4, high_lat, low_lat), low_lat)
    for block, rad_mask in ((0, low_rad), (1, 1.0), (2, high_rad)):
        sides = []
        for slot in range(3):
            right, left = packs[block, 0, slot], packs[block, 1, slot]
            tiles = []
            for spot in range(2 * RAD):
                a = pltpu.roll(right, (LON - GROUP * spot) % LON, 2) if spot else right
                b = pltpu.roll(left, LON - GROUP - GROUP * spot, 2) if spot < 7 else left
                tiles.append(jnp.where((lane < LON // 2)[None], a, b))
            sides.append(tiles)
        for layer in range(RAD):
            high, mid, low = (sides[s][2 * layer:2 * layer + 2] for s in (0, 1, 2))
            columns = (mid[0], mid[1], high[0], jnp.where((sub < 4)[None], high[1], low[0]), low[1])
            at = RAD * block + layer
            for t in range(5):
                mask = tile_masks[t] * rad_mask
                rows = pl.ds(8 * t, 8)
                main = raw[:, at, rows, :]
                ua[at, rows, pl.ds(0, LON)] = main[0] * mask
                ua[at, rows, pl.ds(LON, LON)] = columns[t][0] * mask
                ka[at, rows, pl.ds(0, LON)] = main[1] * (mask * radial_weight)
                ka[at, rows, pl.ds(LON, LON)] = columns[t][1] * (mask * radial_weight)

    def advance(src, dst, depth, pick, lo, hi, sides=None):
        rows = src.shape[1]

        def layer(r):
            if sides is not None and not RAD <= r < 2 * RAD:
                packed = sides[1 if r < RAD else 2]
                turn_by = (LON - 32 * (r % RAD)) % LON
                value = jnp.concatenate([src[r, :, pl.ds(0, LON)], pltpu.roll(packed, turn_by, 1) if turn_by else packed], axis=1)
            else:
                value = src[r]
            if lo is not None and r < RAD:
                value = value * lo
            if hi is not None and r >= 2 * RAD:
                value = value * hi
            return value

        before, here = layer(depth - 1), layer(depth)
        for r in range(depth, 3 * RAD - depth):
            after = layer(r + 1)
            lat = pltpu.roll(here, 1, 0) + pltpu.roll(here, rows - 1, 0)
            lon = pltpu.roll(here, 1, 1) + pltpu.roll(here, 2 * LON - 1, 1)
            dst(r, here + pick(r) * ((before + after) + 3.0 * lat + (5.0 * lon - 18.0 * here)))
            before, here = here, after

    def store(ref):
        def put(r, value):
            ref[r] = value
        return put

    def pick1(r):
        return ka[r]

    def pick2(r):
        return jnp.concatenate([ka[r, pl.ds(0, 24)], ka[r, pl.ds(32, 8)]], axis=0)

    wide_sub = lax.broadcasted_iota(jnp.int32, (8, 2 * LON), 0)

    def pick3(r):
        seam = jnp.where(wide_sub < 4, ka[r, pl.ds(16, 8)], ka[r, pl.ds(32, 8)])
        return jnp.concatenate([ka[r, pl.ds(0, 16)], seam], axis=0)

    def keep2(r, value):
        x2a[r, pl.ds(0, 24)] = value[0:24]
        x2a[r, pl.ds(24, 8)] = value[32:40]

    def keep3(r, value):
        x3a[r, pl.ds(0, 16)] = value[0:16]
        x3a[r, pl.ds(16, 8)] = jnp.where(wide_sub < 4, value[16:24], value[24:32])

    def exchange(ref, side, number):
        main = pl.ds(0, LON)
        for r in (1, -1):
            send(ref.at[own, :, main], ref.at[pl.ds(RAD * block_of(r), RAD), :, main], face_sent.at[number, 0],
                 face_here.at[number, 0], peer(r, 0, 0))
        group = (lax.broadcasted_iota(jnp.int32, side.shape[1:], 1) + GROUP) // 32
        packed = ref[RAD, :, pl.ds(LON, LON)]
        for l in range(1, RAD):
            packed = jnp.where(group == l, pltpu.roll(ref[RAD + l, :, pl.ds(LON, LON)], 32 * l, 1), packed)
        side[0] = packed
        for r in (1, -1):
            send(side.at[0], side.at[1 + block_of(r) // 2], face_sent.at[number, 1], face_here.at[number, 1], peer(r, 0, 0))
        owed.append((ref.at[pl.ds(0, 2 * RAD), :, main], face_sent.at[number, 0]))
        owed.append((side.at[pl.ds(1, 2)], face_sent.at[number, 1]))

    def exchanged(ref, side, number):
        wait_bytes(ref.at[pl.ds(0, 2 * RAD), :, pl.ds(0, LON)], face_here.at[number, 0])
        wait_bytes(side.at[pl.ds(1, 2)], face_here.at[number, 1])

    advance(ua, store(ub), 1, pick1, None, None)
    advance(ub, store(ua), 2, pick1, None, None)
    advance(ua, store(ub), 3, pick1, None, None)
    advance(ub, keep2, 4, pick1, None, None)
    exchange(x2a, side2, 0)
    pl.semaphore_wait(near_in, len(outer))
    for r in (-4, 4):
        pl.semaphore_signal(far_in, inc=1, device_id=peer(r, 0, 0), device_id_type=MESH)
    gram_start(1)
    exchanged(x2a, side2, 0)
    advance(x2a, store(x2b), 1, pick2, low_rad, high_rad, side2)
    advance(x2b, store(x2c), 2, pick2, None, None)
    advance(x2c, store(x2b), 3, pick2, None, None)
    advance(x2b, keep3, 4, pick2, None, None)
    exchange(x3a, side3, 1)
    gram_send[1, lines] = gram_end(1)
    gram_start(2)

    def spread(src, dst, step):
        first, last = RAD - step, 2 * RAD - 1 + step

        def layer(r):
            return src[r] if first < r < last else None

        def plus(a, b):
            return b if a is None else a if b is None else a + b

        for r in range(first, last + 1):
            here, around = layer(r), plus(layer(r - 1), layer(r + 1))
            if here is None:
                dst[r] = pick3(r) * around
                continue
            lat = pltpu.roll(here, 1, 0) + pltpu.roll(here, here.shape[0] - 1, 0)
            lon = pltpu.roll(here, 1, 1) + pltpu.roll(here, 2 * LON - 1, 1)
            dst[r] = here + pick3(r) * (around + 3.0 * lat + (5.0 * lon - 18.0 * here))

    spread(x3a, va, 1)
    spread(va, vb, 2)
    spread(vb, va, 3)
    spread(va, vb, 4)

    wait_bytes(near_hist, hist_here)
    acc = [jnp.zeros((pairs, 8, LON), F32) for _ in range(2)]
    for r in range(3 * RAD):
        for half in range(LAT // 8):
            rows = pl.ds(8 * half, 8)
            field = vb[r, rows, pl.ds(0, LON)][None]
            for h in range(2):
                if RAD <= r < 2 * RAD:
                    values = hist[h, :, r - RAD, rows, :]
                else:
                    values = near_hist[r // (2 * RAD), h, :, r % RAD, rows, :]
                acc[h] = acc[h] + values * field
    line = jnp.zeros((8, LON), F32)
    for h in range(2):
        sums = jnp.sum(acc[h], axis=2, keepdims=True)
        for i in range(pairs):
            line = jnp.where(lane == GROUP * h + i, sums[i], line)

    def hops(offset):
        return sum(min(d, n - d) for d, n in zip(offset, sizes))

    def add_up(buf, row, offsets, number):
        count = len(offsets)
        buf[pl.ds(count, 1)] = row
        for at, offset in enumerate(sorted(offsets, key=lambda c: -hops(c))):
            send(buf.at[pl.ds(count, 1)], buf.at[pl.ds(at, 1)], row_sent.at[number], row_here.at[number], peer(*offset))
        owed.append((buf.at[pl.ds(0, count)], row_sent.at[number]))

    def added(buf, offsets, number):
        count = len(offsets)
        wait_bytes(buf.at[pl.ds(0, count)], row_here.at[number])
        return jnp.sum(buf[pl.ds(0, count + 1)], axis=0, keepdims=True)

    in_plane = [(0, a, o) for a in range(n_lat) for o in range(n_lon)][1:]
    in_rad = [(r, 0, 0) for r in range(1, n_rad)]
    add_up(plane_row, jnp.sum(line, axis=0, keepdims=True), in_plane, 0)
    pl.semaphore_wait(far_in, 2)
    gram_send[2, lines] = gram_end(2)
    gram_start(0)
    exchanged(x3a, side3, 1)
    advance(x3a, store(x3b), 1, pick3, low_rad, high_rad, side3)
    advance(x3b, store(x3c), 2, pick3, None, None)
    advance(x3c, store(x3b), 3, pick3, None, None)

    def finish(r, value):
        minus_smooth[r - RAD] = -value[0:LAT, 0:LON]

    advance(x3b, finish, 4, pick3, None, None)

    add_up(rad_row, added(plane_row, in_plane, 0), in_rad, 1)

    packed = gram_end(0)
    parts = [pltpu.roll(packed[i // 4:i // 4 + 1], LON - 32 * (i % 4), 1) if i % 4 else packed[i // 4:i // 4 + 1]
             for i in range(pairs)]
    gram = jnp.concatenate(parts + [jnp.zeros((16 - pairs, LON), F32)], axis=0)
    col = lax.broadcasted_iota(jnp.int32, (16, LON), 1)
    row = lax.broadcasted_iota(jnp.int32, (16, LON), 0)
    inside = row < pairs
    diagonal = (col == row) & inside
    d = jnp.sum(jnp.where(diagonal, gram, 0.0), axis=1, keepdims=True)
    inverse = 1.0 / jnp.where(inside[:, 0:1], d, 1.0)
    scaling = gram[pairs - 1:pairs, pairs - 1:pairs] / gram[pairs - 1:pairs, GROUP + pairs - 1:GROUP + pairs]
    upper = jnp.where((col > row) & (col < pairs), gram * inverse, 0.0)
    solve = jnp.where(diagonal, 1.0, 0.0)
    for k in range(pairs - 1, 0, -1):
        solve = solve - upper[:, k:k + 1] * solve[k:k + 1, :]
    inverse_row = jnp.sum(jnp.where(diagonal, inverse, 0.0), axis=0, keepdims=True)
    alpha = solve * inverse_row
    right = d * alpha
    for k in range(pairs):
        right = right + (scaling * gram[:, GROUP + k:GROUP + k + 1]) * alpha[k:k + 1, :]
    right = jnp.where((col == row + GROUP) & inside, -scaling, right)
    for k in range(pairs - 1):
        column = jnp.sum(jnp.where(col == row, upper[k:k + 1, :], 0.0), axis=1, keepdims=True)
        right = right - column * right[k:k + 1, :]
    of_s = right * inverse
    of_y = -scaling * alpha

    b = added(rad_row, in_rad, 1)
    coef[0] = jnp.broadcast_to(jnp.sum(of_s * b, axis=1, keepdims=True), (16, LON))
    coef[1] = jnp.broadcast_to(jnp.sum(of_y * b, axis=1, keepdims=True), (16, LON))
    for spot in range(2 * RAD):
        rows = pl.ds(8 * (spot % 2), 8)
        value = -scaling * minus_smooth[spot // 2, rows, :]
        for i in range(pairs):
            value = value + coef[0, pl.ds(i, 1)] * hist[0, i, spot // 2, rows, :]
            value = value + coef[1, pl.ds(i, 1)] * hist[1, i, spot // 2, rows, :]
        minus_dir[spot // 2, rows, :] = value

    for ref, sem in owed:
        wait_bytes(ref, sem)


def per_device(sizes, gradient, conductance, s_hist, y_hist):
    pairs = s_hist.shape[0]
    most = max(sizes)
    vmem, dma = pltpu.VMEM, pltpu.SemaphoreType.DMA
    inputs = [pltpu.with_memory_space_constraint(a, pltpu.HBM) for a in (gradient, conductance, s_hist, y_hist)]
    out = pl.pallas_call(
        functools.partial(kernel, sizes),
        out_shape=pltpu.VMEM((2,) + gradient.shape, F32),
        in_specs=[pl.BlockSpec(memory_space=pltpu.HBM)] * 4,
        out_specs=pl.BlockSpec(memory_space=vmem),
        scratch_shapes=[
            vmem((2, 3 * RAD, 40, LON), F32),
            vmem((2, pairs, RAD, LAT, LON), F32),
            vmem((2, 2, 8, LON), F32),
            vmem((3, 2, 3, 2, 8, LON), F32),
            vmem((3 * RAD, 40, 2 * LON), F32),
            vmem((3 * RAD, 40, 2 * LON), F32),
            vmem((3 * RAD, 40, 2 * LON), F32),
            vmem((3 * RAD, 32, 2 * LON), F32),
            vmem((3 * RAD, 32, 2 * LON), F32),
            vmem((3 * RAD, 32, 2 * LON), F32),
            vmem((3 * RAD, 24, 2 * LON), F32),
            vmem((3 * RAD, 24, 2 * LON), F32),
            vmem((3 * RAD, 24, 2 * LON), F32),
            vmem((3, 32, LON), F32),
            vmem((3, 24, LON), F32),
            vmem((3 * RAD, 24, 2 * LON), F32),
            vmem((3 * RAD, 24, 2 * LON), F32),
            vmem((2, 2, pairs, RAD, LAT, LON), F32),
            vmem((3, 8, LON), F32),
            vmem((3, most - 1, 8, LON), F32),
            vmem((sizes[1] * sizes[2], LON), F32),
            vmem((sizes[0], LON), F32),
            vmem((2, 16, LON), F32),
            dma((4,)),
            dma((4,)),
            dma((4,)),
            dma((2, 2)),
            dma((2, 2)),
            dma((3,)),
            dma((3,)),
            dma((2,)),
            dma((2,)),
            pltpu.SemaphoreType.DMA,
            pltpu.SemaphoreType.DMA,
            pltpu.SemaphoreType.REGULAR,
            pltpu.SemaphoreType.REGULAR,
        ],
        compiler_params=pltpu.CompilerParams(collective_id=0, has_side_effects=True, vmem_limit_bytes=24 * 2**20),
        cost_estimate=pl.CostEstimate(flops=20_000_000, bytes_accessed=800_000, transcendentals=0),
        name="filter_and_direction",
    )(*inputs)
    return -out[0], -out[1]


def solution(mesh):
    sizes = tuple(mesh.shape[a] for a in AXES)
    field, history = P(*AXES), P(None, *AXES)
    return jax.shard_map(
        functools.partial(per_device, sizes),
        mesh=mesh,
        in_specs=(field, field, history, history),
        out_specs=(field, field),
        check_vma=False,
    )
```

```python
import functools

import jax
import jax.numpy as jnp
from jax import lax
from jax.experimental import pallas as pl
from jax.experimental.pallas import tpu as pltpu
from jax.sharding import PartitionSpec as P

STEPS = 12
AXES = ("rad", "lat", "lon")
MESH = pl.DeviceIdType.MESH

RAD, LAT, LON = 4, 16, 128
WIDE = 12
GROUP = 16
radial_weight = 0.05
latitude_weight = 0.15
longitude_weight = 0.25
F32 = jnp.float32


def ordered(n):
    return sorted(range(1, n), key=lambda d: -min(d, n - d))


def kernel(sizes, g_hbm, k_hbm, s_hbm, y_hbm, out_ref, raw, hist, edges, packs, ua, ka, ub, x2a, x2b, x2c, x3a,
           x3b, x3c, side2, side3, va, vb, near_hist, gram_send, gram_recv, plane_row, rad_row, coef, load_sem, halo_sent, halo_here, face_sent, face_here,
           gram_sent, gram_here, row_sent, row_here, hist_sent, hist_here, near_in, far_in):
    n_rad, n_lat, n_lon = sizes
    pairs = s_hbm.shape[0]
    minus_smooth, minus_dir = out_ref.at[0], out_ref.at[1]
    me = tuple(lax.axis_index(a) for a in AXES)

    def peer(*offset):
        return tuple(lax.rem(m + (o % n), n) if o % n else m for m, o, n in zip(me, offset, sizes))

    owed = []

    def send(src, dst, ssem, rsem, target):
        pltpu.make_async_remote_copy(src_ref=src, dst_ref=dst, send_sem=ssem, recv_sem=rsem, device_id=target,
                                     device_id_type=MESH).start()

    def wait_bytes(ref, sem):
        pltpu.make_async_copy(ref, ref, sem).wait()

    load_g = pltpu.make_async_copy(g_hbm, raw.at[0, pl.ds(RAD, RAD), pl.ds(0, LAT)], load_sem.at[0])
    load_k = pltpu.make_async_copy(k_hbm, raw.at[1, pl.ds(RAD, RAD), pl.ds(0, LAT)], load_sem.at[1])
    load_s = pltpu.make_async_copy(s_hbm, hist.at[0], load_sem.at[2])
    load_y = pltpu.make_async_copy(y_hbm, hist.at[1], load_sem.at[3])
    for copy in (load_g, load_k, load_s, load_y):
        copy.start()

    near = (0, -1, 1)
    cube = [(r, a, o) for r in near for a in near for o in near][1:]
    cube.sort(key=lambda c: -sum(map(abs, c)))
    partners = cube + [(-2, 0, 0), (2, 0, 0)]
    barrier = pltpu.get_barrier_semaphore()
    for offset in partners:
        pl.semaphore_signal(barrier, inc=1, device_id=peer(*offset), device_id_type=MESH)

    lane = lax.broadcasted_iota(jnp.int32, (8, LON), 1)
    sub = lax.broadcasted_iota(jnp.int32, (8, LON), 0)

    load_g.wait()
    load_k.wait()
    to_right = jnp.zeros((2, 8, LON), F32)
    to_left = jnp.zeros((2, 8, LON), F32)
    for spot in range(2 * RAD):
        tile = raw[:, RAD + spot // 2, pl.ds(8 * (spot % 2), 8), :]
        here = (lane // GROUP == spot)[None]
        to_right = jnp.where(here, pltpu.roll(tile, (GROUP * spot + GROUP) % LON, 2), to_right)
        to_left = jnp.where(here, pltpu.roll(tile, GROUP * spot, 2) if spot else tile, to_left)
    edges[0] = to_left
    edges[1] = to_right

    pl.semaphore_wait(barrier, len(partners))

    own = pl.ds(RAD, RAD)

    def block_of(r):
        return 1 - r

    rows_of = {-1: (0, WIDE, LAT), 0: (0, LAT, 0), 1: (LAT - WIDE, WIDE, LAT + WIDE)}

    def halo(r, a, o):
        at = block_of(r)
        if o:
            side = (o + 1) // 2
            send(edges.at[side], packs.at[at, side, 1 + a], halo_sent.at[3], halo_here.at[3], peer(r, a, o))
        else:
            first, count, to = rows_of[a]
            send(raw.at[:, own, pl.ds(first, count)], raw.at[:, pl.ds(RAD * at, RAD), pl.ds(to, count)], halo_sent.at[at],
                 halo_here.at[at], peer(r, a, o))

    for offset in cube:
        halo(*offset)
    halos = ((raw.at[:, pl.ds(0, RAD)], 0), (raw.at[:, own, pl.ds(LAT, 2 * WIDE)], 1), (raw.at[:, pl.ds(2 * RAD, RAD)], 2),
             (packs, 3))
    owed += [(ref, halo_sent.at[number]) for ref, number in halos]

    load_s.wait()
    load_y.wait()
    odd = lax.rem(me[0], 2)

    def along(step):
        return (lax.rem(me[0] + step + n_rad, n_rad), me[1], me[2])

    send(hist, near_hist.at[odd], hist_sent.at[0], hist_here.at[0], along(1 - 2 * odd))
    send(hist.at[0], near_hist.at[1 - odd, 0], hist_sent.at[1], hist_here.at[1], along(2 * odd - 1))
    owed += [(near_hist.at[0], hist_sent.at[0]), (near_hist.at[1], hist_sent.at[1])]

    def pass_on():
        wait_bytes(near_hist.at[0], hist_here.at[0])
        send(near_hist.at[1 - odd, 1], near_hist.at[odd, 1], hist_sent.at[1], hist_here.at[1], along(2 - 4 * odd))

    total = [jnp.zeros((8, LON), F32) for _ in range(-(-pairs // 4))]
    for j in range(pairs):
        if j == pairs // 2:
            pass_on()
        acc_s = jnp.zeros((pairs, 8, LON), F32)
        acc_y = jnp.zeros((pairs, 8, LON), F32)
        for spot in range(2 * RAD):
            rows = pl.ds(8 * (spot % 2), 8)
            one = hist[1, j, spot // 2, rows, :][None]
            acc_s += hist[0, :, spot // 2, rows, :] * one
            acc_y += hist[1, :, spot // 2, rows, :] * one
        sum_s = jnp.sum(acc_s, axis=2, keepdims=True)
        sum_y = jnp.sum(acc_y, axis=2, keepdims=True)
        for i in range(pairs):
            at = 32 * (i % 4) + j
            total[i // 4] = jnp.where(lane == at, sum_s[i], jnp.where(lane == at + GROUP, sum_y[i], total[i // 4]))
    for line, value in enumerate(total):
        gram_send[0, pl.ds(line, 1)] = jnp.sum(value, axis=0, keepdims=True)
    lines = pl.ds(0, len(total))

    for ref, number in halos:
        wait_bytes(ref, halo_here.at[number])

    signs = (0, -2, 2)
    outer = [(0, a, o) for a in signs for o in signs][1:] + [(-2, 0, 0), (2, 0, 0)]
    for offset in outer:
        pl.semaphore_signal(near_in, inc=1, device_id=peer(*offset), device_id_type=MESH)

    turn = {1: 0, 2: 1, 0: 2}

    def gram_start(stage):
        at = turn[stage]
        for d in ordered(sizes[stage]):
            offset = [0, 0, 0]
            offset[stage] = d
            send(gram_send.at[at, lines], gram_recv.at[at, d - 1, lines], gram_sent.at[at], gram_here.at[at], peer(*offset))
        owed.append((gram_recv.at[at, pl.ds(0, sizes[stage] - 1), lines], gram_sent.at[at]))

    def gram_end(stage):
        at = turn[stage]
        ref = gram_recv.at[at, pl.ds(0, sizes[stage] - 1), lines]
        wait_bytes(ref, gram_here.at[at])
        return gram_send[at, lines] + jnp.sum(gram_recv[at, pl.ds(0, sizes[stage] - 1), lines], axis=0)

    low_rad = (me[0] > 0).astype(F32)
    high_rad = (me[0] < n_rad - 1).astype(F32)
    low_lat = (me[1] > 0).astype(F32)
    high_lat = (me[1] < n_lat - 1).astype(F32)
    tile_masks = (1.0, 1.0, high_lat, jnp.where(sub < 4, high_lat, low_lat), low_lat)
    for block, rad_mask in ((0, low_rad), (1, 1.0), (2, high_rad)):
        sides = []
        for slot in range(3):
            right, left = packs[block, 0, slot], packs[block, 1, slot]
            tiles = []
            for spot in range(2 * RAD):
                a = pltpu.roll(right, (LON - GROUP * spot) % LON, 2) if spot else right
                b = pltpu.roll(left, LON - GROUP - GROUP * spot, 2) if spot < 7 else left
                tiles.append(jnp.where((lane < LON // 2)[None], a, b))
            sides.append(tiles)
        for layer in range(RAD):
            high, mid, low = (sides[s][2 * layer:2 * layer + 2] for s in (0, 1, 2))
            columns = (mid[0], mid[1], high[0], jnp.where((sub < 4)[None], high[1], low[0]), low[1])
            at = RAD * block + layer
            for t in range(5):
                mask = tile_masks[t] * rad_mask
                rows = pl.ds(8 * t, 8)
                main = raw[:, at, rows, :]
                ua[at, rows, pl.ds(0, LON)] = main[0] * mask
                ua[at, rows, pl.ds(LON, LON)] = columns[t][0] * mask
                ka[at, rows, pl.ds(0, LON)] = main[1] * (mask * radial_weight)
                ka[at, rows, pl.ds(LON, LON)] = columns[t][1] * (mask * radial_weight)

    def advance(src, dst, depth, pick, lo, hi, sides=None):
        rows = src.shape[1]

        def layer(r):
            if sides is not None and not RAD <= r < 2 * RAD:
                packed = sides[1 if r < RAD else 2]
                turn_by = (LON - 32 * (r % RAD)) % LON
                value = jnp.concatenate([src[r, :, pl.ds(0, LON)], pltpu.roll(packed, turn_by, 1) if turn_by else packed], axis=1)
            else:
                value = src[r]
            if lo is not None and r < RAD:
                value = value * lo
            if hi is not None and r >= 2 * RAD:
                value = value * hi
            return value

        before, here = layer(depth - 1), layer(depth)
        for r in range(depth, 3 * RAD - depth):
            after = layer(r + 1)
            lat = pltpu.roll(here, 1, 0) + pltpu.roll(here, rows - 1, 0)
            lon = pltpu.roll(here, 1, 1) + pltpu.roll(here, 2 * LON - 1, 1)
            dst(r, here + pick(r) * ((before + after) + 3.0 * lat + (5.0 * lon - 18.0 * here)))
            before, here = here, after

    def store(ref):
        def put(r, value):
            ref[r] = value
        return put

    def pick1(r):
        return ka[r]

    def pick2(r):
        return jnp.concatenate([ka[r, pl.ds(0, 24)], ka[r, pl.ds(32, 8)]], axis=0)

    wide_sub = lax.broadcasted_iota(jnp.int32, (8, 2 * LON), 0)

    def pick3(r):
        seam = jnp.where(wide_sub < 4, ka[r, pl.ds(16, 8)], ka[r, pl.ds(32, 8)])
        return jnp.concatenate([ka[r, pl.ds(0, 16)], seam], axis=0)

    def keep2(r, value):
        x2a[r, pl.ds(0, 24)] = value[0:24]
        x2a[r, pl.ds(24, 8)] = value[32:40]

    def keep3(r, value):
        x3a[r, pl.ds(0, 16)] = value[0:16]
        x3a[r, pl.ds(16, 8)] = jnp.where(wide_sub < 4, value[16:24], value[24:32])

    def exchange(ref, side, number):
        main = pl.ds(0, LON)
        for r in (1, -1):
            send(ref.at[own, :, main], ref.at[pl.ds(RAD * block_of(r), RAD), :, main], face_sent.at[number, 0],
                 face_here.at[number, 0], peer(r, 0, 0))
        group = (lax.broadcasted_iota(jnp.int32, side.shape[1:], 1) + GROUP) // 32
        packed = ref[RAD, :, pl.ds(LON, LON)]
        for l in range(1, RAD):
            packed = jnp.where(group == l, pltpu.roll(ref[RAD + l, :, pl.ds(LON, LON)], 32 * l, 1), packed)
        side[0] = packed
        for r in (1, -1):
            send(side.at[0], side.at[1 + block_of(r) // 2], face_sent.at[number, 1], face_here.at[number, 1], peer(r, 0, 0))
        owed.append((ref.at[pl.ds(0, 2 * RAD), :, main], face_sent.at[number, 0]))
        owed.append((side.at[pl.ds(1, 2)], face_sent.at[number, 1]))

    def exchanged(ref, side, number):
        wait_bytes(ref.at[pl.ds(0, 2 * RAD), :, pl.ds(0, LON)], face_here.at[number, 0])
        wait_bytes(side.at[pl.ds(1, 2)], face_here.at[number, 1])

    advance(ua, store(ub), 1, pick1, None, None)
    advance(ub, store(ua), 2, pick1, None, None)
    advance(ua, store(ub), 3, pick1, None, None)
    advance(ub, keep2, 4, pick1, None, None)
    exchange(x2a, side2, 0)
    pl.semaphore_wait(near_in, len(outer))
    for r in (-4, 4):
        pl.semaphore_signal(far_in, inc=1, device_id=peer(r, 0, 0), device_id_type=MESH)
    gram_start(1)
    exchanged(x2a, side2, 0)
    advance(x2a, store(x2b), 1, pick2, low_rad, high_rad, side2)
    advance(x2b, store(x2c), 2, pick2, None, None)
    advance(x2c, store(x2b), 3, pick2, None, None)
    advance(x2b, keep3, 4, pick2, None, None)
    exchange(x3a, side3, 1)
    gram_send[1, lines] = gram_end(1)
    gram_start(2)

    def spread(src, dst, step):
        first, last = RAD - step, 2 * RAD - 1 + step

        def layer(r):
            return src[r] if first < r < last else None

        def plus(a, b):
            return b if a is None else a if b is None else a + b

        for r in range(first, last + 1):
            here, around = layer(r), plus(layer(r - 1), layer(r + 1))
            if here is None:
                dst[r] = pick3(r) * around
                continue
            lat = pltpu.roll(here, 1, 0) + pltpu.roll(here, here.shape[0] - 1, 0)
            lon = pltpu.roll(here, 1, 1) + pltpu.roll(here, 2 * LON - 1, 1)
            dst[r] = here + pick3(r) * (around + 3.0 * lat + (5.0 * lon - 18.0 * here))

    spread(x3a, va, 1)
    spread(va, vb, 2)
    spread(vb, va, 3)
    spread(va, vb, 4)

    wait_bytes(near_hist.at[1], hist_here.at[1])
    acc = [jnp.zeros((pairs, 8, LON), F32) for _ in range(2)]
    for r in range(3 * RAD):
        for half in range(LAT // 8):
            rows = pl.ds(8 * half, 8)
            field = vb[r, rows, pl.ds(0, LON)][None]
            for h in range(2):
                if RAD <= r < 2 * RAD:
                    values = hist[h, :, r - RAD, rows, :]
                else:
                    values = near_hist[r // (2 * RAD), h, :, r % RAD, rows, :]
                acc[h] = acc[h] + values * field
    line = jnp.zeros((8, LON), F32)
    for h in range(2):
        sums = jnp.sum(acc[h], axis=2, keepdims=True)
        for i in range(pairs):
            line = jnp.where(lane == GROUP * h + i, sums[i], line)

    def hops(offset):
        return sum(min(d, n - d) for d, n in zip(offset, sizes))

    def add_up(buf, row, offsets, number):
        count = len(offsets)
        buf[pl.ds(count, 1)] = row
        for at, offset in enumerate(sorted(offsets, key=lambda c: -hops(c))):
            send(buf.at[pl.ds(count, 1)], buf.at[pl.ds(at, 1)], row_sent.at[number], row_here.at[number], peer(*offset))
        owed.append((buf.at[pl.ds(0, count)], row_sent.at[number]))

    def added(buf, offsets, number):
        count = len(offsets)
        wait_bytes(buf.at[pl.ds(0, count)], row_here.at[number])
        return jnp.sum(buf[pl.ds(0, count + 1)], axis=0, keepdims=True)

    in_plane = [(0, a, o) for a in range(n_lat) for o in range(n_lon)][1:]
    in_rad = [(r, 0, 0) for r in range(1, n_rad)]
    add_up(plane_row, jnp.sum(line, axis=0, keepdims=True), in_plane, 0)
    pl.semaphore_wait(far_in, 2)
    gram_send[2, lines] = gram_end(2)
    gram_start(0)
    exchanged(x3a, side3, 1)
    advance(x3a, store(x3b), 1, pick3, low_rad, high_rad, side3)
    advance(x3b, store(x3c), 2, pick3, None, None)
    advance(x3c, store(x3b), 3, pick3, None, None)

    def finish(r, value):
        minus_smooth[r - RAD] = -value[0:LAT, 0:LON]

    advance(x3b, finish, 4, pick3, None, None)

    add_up(rad_row, added(plane_row, in_plane, 0), in_rad, 1)

    packed = gram_end(0)
    parts = [pltpu.roll(packed[i // 4:i // 4 + 1], LON - 32 * (i % 4), 1) if i % 4 else packed[i // 4:i // 4 + 1]
             for i in range(pairs)]
    gram = jnp.concatenate(parts + [jnp.zeros((16 - pairs, LON), F32)], axis=0)
    col = lax.broadcasted_iota(jnp.int32, (16, LON), 1)
    row = lax.broadcasted_iota(jnp.int32, (16, LON), 0)
    inside = row < pairs
    diagonal = (col == row) & inside
    d = jnp.sum(jnp.where(diagonal, gram, 0.0), axis=1, keepdims=True)
    inverse = 1.0 / jnp.where(inside[:, 0:1], d, 1.0)
    scaling = gram[pairs - 1:pairs, pairs - 1:pairs] / gram[pairs - 1:pairs, GROUP + pairs - 1:GROUP + pairs]
    upper = jnp.where((col > row) & (col < pairs), gram * inverse, 0.0)
    solve = jnp.where(diagonal, 1.0, 0.0)
    for k in range(pairs - 1, 0, -1):
        solve = solve - upper[:, k:k + 1] * solve[k:k + 1, :]
    inverse_row = jnp.sum(jnp.where(diagonal, inverse, 0.0), axis=0, keepdims=True)
    alpha = solve * inverse_row
    right = d * alpha
    for k in range(pairs):
        right = right + (scaling * gram[:, GROUP + k:GROUP + k + 1]) * alpha[k:k + 1, :]
    right = jnp.where((col == row + GROUP) & inside, -scaling, right)
    for k in range(pairs - 1):
        column = jnp.sum(jnp.where(col == row, upper[k:k + 1, :], 0.0), axis=1, keepdims=True)
        right = right - column * right[k:k + 1, :]
    of_s = right * inverse
    of_y = -scaling * alpha

    b = added(rad_row, in_rad, 1)
    coef[0] = jnp.broadcast_to(jnp.sum(of_s * b, axis=1, keepdims=True), (16, LON))
    coef[1] = jnp.broadcast_to(jnp.sum(of_y * b, axis=1, keepdims=True), (16, LON))
    for spot in range(2 * RAD):
        rows = pl.ds(8 * (spot % 2), 8)
        value = -scaling * minus_smooth[spot // 2, rows, :]
        for i in range(pairs):
            value = value + coef[0, pl.ds(i, 1)] * hist[0, i, spot // 2, rows, :]
            value = value + coef[1, pl.ds(i, 1)] * hist[1, i, spot // 2, rows, :]
        minus_dir[spot // 2, rows, :] = value

    for ref, sem in owed:
        wait_bytes(ref, sem)


def per_device(sizes, gradient, conductance, s_hist, y_hist):
    pairs = s_hist.shape[0]
    most = max(sizes)
    vmem, dma = pltpu.VMEM, pltpu.SemaphoreType.DMA
    inputs = [pltpu.with_memory_space_constraint(a, pltpu.HBM) for a in (gradient, conductance, s_hist, y_hist)]
    out = pl.pallas_call(
        functools.partial(kernel, sizes),
        out_shape=pltpu.VMEM((2,) + gradient.shape, F32),
        in_specs=[pl.BlockSpec(memory_space=pltpu.HBM)] * 4,
        out_specs=pl.BlockSpec(memory_space=vmem),
        scratch_shapes=[
            vmem((2, 3 * RAD, 40, LON), F32),
            vmem((2, pairs, RAD, LAT, LON), F32),
            vmem((2, 2, 8, LON), F32),
            vmem((3, 2, 3, 2, 8, LON), F32),
            vmem((3 * RAD, 40, 2 * LON), F32),
            vmem((3 * RAD, 40, 2 * LON), F32),
            vmem((3 * RAD, 40, 2 * LON), F32),
            vmem((3 * RAD, 32, 2 * LON), F32),
            vmem((3 * RAD, 32, 2 * LON), F32),
            vmem((3 * RAD, 32, 2 * LON), F32),
            vmem((3 * RAD, 24, 2 * LON), F32),
            vmem((3 * RAD, 24, 2 * LON), F32),
            vmem((3 * RAD, 24, 2 * LON), F32),
            vmem((3, 32, LON), F32),
            vmem((3, 24, LON), F32),
            vmem((3 * RAD, 24, 2 * LON), F32),
            vmem((3 * RAD, 24, 2 * LON), F32),
            vmem((2, 2, pairs, RAD, LAT, LON), F32),
            vmem((3, 8, LON), F32),
            vmem((3, most - 1, 8, LON), F32),
            vmem((sizes[1] * sizes[2], LON), F32),
            vmem((sizes[0], LON), F32),
            vmem((2, 16, LON), F32),
            dma((4,)),
            dma((4,)),
            dma((4,)),
            dma((2, 2)),
            dma((2, 2)),
            dma((3,)),
            dma((3,)),
            dma((2,)),
            dma((2,)),
            dma((2,)),
            dma((2,)),
            pltpu.SemaphoreType.REGULAR,
            pltpu.SemaphoreType.REGULAR,
        ],
        compiler_params=pltpu.CompilerParams(collective_id=0, has_side_effects=True, vmem_limit_bytes=24 * 2**20),
        cost_estimate=pl.CostEstimate(flops=20_000_000, bytes_accessed=800_000, transcendentals=0),
        name="filter_and_direction",
    )(*inputs)
    return -out[0], -out[1]


def solution(mesh):
    sizes = tuple(mesh.shape[a] for a in AXES)
    field, history = P(*AXES), P(None, *AXES)
    return jax.shard_map(
        functools.partial(per_device, sizes),
        mesh=mesh,
        in_specs=(field, field, history, history),
        out_specs=(field, field),
        check_vma=False,
    )
```

```python
import functools

import jax
import jax.numpy as jnp
from jax import lax
from jax.experimental import pallas as pl
from jax.experimental.pallas import tpu as pltpu
from jax.sharding import PartitionSpec as P

STEPS = 12
AXES = ("rad", "lat", "lon")
MESH = pl.DeviceIdType.MESH

RAD, LAT, LON = 4, 16, 128
WIDE = 12
GROUP = 16
radial_weight = 0.05
latitude_weight = 0.15
longitude_weight = 0.25
F32 = jnp.float32


def ordered(n):
    return sorted(range(1, n), key=lambda d: -min(d, n - d))


def kernel(sizes, g_hbm, k_hbm, s_hbm, y_hbm, out_ref, raw, hist, edges, packs, ua, ka, ub, x2a, x2b, x2c, x3a,
           x3b, x3c, side2, side3, gram_send, gram_recv, plane_row, rad_row, coef, load_sem, halo_sent, halo_here, face_sent, face_here,
           gram_sent, gram_here, row_sent, row_here, near_in, far_in):
    n_rad, n_lat, n_lon = sizes
    pairs = s_hbm.shape[0]
    minus_smooth, minus_dir = out_ref.at[0], out_ref.at[1]
    me = tuple(lax.axis_index(a) for a in AXES)

    def peer(*offset):
        return tuple(lax.rem(m + (o % n), n) if o % n else m for m, o, n in zip(me, offset, sizes))

    owed = []

    def send(src, dst, ssem, rsem, target):
        pltpu.make_async_remote_copy(src_ref=src, dst_ref=dst, send_sem=ssem, recv_sem=rsem, device_id=target,
                                     device_id_type=MESH).start()

    def drain():
        while owed:
            wait_bytes(*owed.pop())

    def wait_bytes(ref, sem):
        pltpu.make_async_copy(ref, ref, sem).wait()

    near = (0, -1, 1)
    cube = [(r, a, o) for r in near for a in near for o in near][1:]
    cube.sort(key=lambda c: -sum(map(abs, c)))
    barrier = pltpu.get_barrier_semaphore()
    for offset in cube:
        pl.semaphore_signal(barrier, inc=1, device_id=peer(*offset), device_id_type=MESH)

    load_g = pltpu.make_async_copy(g_hbm, raw.at[0, pl.ds(RAD, RAD), pl.ds(0, LAT)], load_sem.at[0])
    load_k = pltpu.make_async_copy(k_hbm, raw.at[1, pl.ds(RAD, RAD), pl.ds(0, LAT)], load_sem.at[1])
    load_s = pltpu.make_async_copy(s_hbm, hist.at[0], load_sem.at[2])
    load_y = pltpu.make_async_copy(y_hbm, hist.at[1], load_sem.at[3])
    for copy in (load_g, load_k, load_s, load_y):
        copy.start()

    lane = lax.broadcasted_iota(jnp.int32, (8, LON), 1)
    sub = lax.broadcasted_iota(jnp.int32, (8, LON), 0)

    load_g.wait()
    load_k.wait()
    to_right = jnp.zeros((2, 8, LON), F32)
    to_left = jnp.zeros((2, 8, LON), F32)
    for spot in range(2 * RAD):
        tile = raw[:, RAD + spot // 2, pl.ds(8 * (spot % 2), 8), :]
        here = (lane // GROUP == spot)[None]
        to_right = jnp.where(here, pltpu.roll(tile, (GROUP * spot + GROUP) % LON, 2), to_right)
        to_left = jnp.where(here, pltpu.roll(tile, GROUP * spot, 2) if spot else tile, to_left)
    edges[0] = to_left
    edges[1] = to_right

    pl.semaphore_wait(barrier, len(cube))

    own = pl.ds(RAD, RAD)

    def block_of(r):
        return 1 - r

    rows_of = {-1: (0, WIDE, LAT), 0: (0, LAT, 0), 1: (LAT - WIDE, WIDE, LAT + WIDE)}

    def halo(r, a, o):
        at = block_of(r)
        if o:
            side = (o + 1) // 2
            send(edges.at[side], packs.at[at, side, 1 + a], halo_sent.at[3], halo_here.at[3], peer(r, a, o))
        else:
            first, count, to = rows_of[a]
            send(raw.at[:, own, pl.ds(first, count)], raw.at[:, pl.ds(RAD * at, RAD), pl.ds(to, count)], halo_sent.at[at],
                 halo_here.at[at], peer(r, a, o))

    for offset in cube:
        halo(*offset)
    halos = ((raw.at[:, pl.ds(0, RAD)], 0), (raw.at[:, own, pl.ds(LAT, 2 * WIDE)], 1), (raw.at[:, pl.ds(2 * RAD, RAD)], 2),
             (packs, 3))
    owed += [(ref, halo_sent.at[number]) for ref, number in halos]

    load_s.wait()
    load_y.wait()
    total = [jnp.zeros((8, LON), F32) for _ in range(-(-pairs // 4))]
    for j in range(pairs):
        acc_s = jnp.zeros((pairs, 8, LON), F32)
        acc_y = jnp.zeros((pairs, 8, LON), F32)
        for spot in range(2 * RAD):
            rows = pl.ds(8 * (spot % 2), 8)
            one = hist[1, j, spot // 2, rows, :][None]
            acc_s += hist[0, :, spot // 2, rows, :] * one
            acc_y += hist[1, :, spot // 2, rows, :] * one
        sum_s = jnp.sum(acc_s, axis=2, keepdims=True)
        sum_y = jnp.sum(acc_y, axis=2, keepdims=True)
        for i in range(pairs):
            at = 32 * (i % 4) + j
            total[i // 4] = jnp.where(lane == at, sum_s[i], jnp.where(lane == at + GROUP, sum_y[i], total[i // 4]))
    for line, value in enumerate(total):
        gram_send[0, pl.ds(line, 1)] = jnp.sum(value, axis=0, keepdims=True)
    lines = pl.ds(0, len(total))

    for ref, number in halos:
        wait_bytes(ref, halo_here.at[number])

    signs = (0, -2, 2)
    outer = [(0, a, o) for a in signs for o in signs][1:] + [(-2, 0, 0), (2, 0, 0)]
    for offset in outer:
        pl.semaphore_signal(near_in, inc=1, device_id=peer(*offset), device_id_type=MESH)

    turn = {1: 0, 2: 1, 0: 2}

    def gram_start(stage):
        at = turn[stage]
        for d in ordered(sizes[stage]):
            offset = [0, 0, 0]
            offset[stage] = d
            send(gram_send.at[at, lines], gram_recv.at[at, d - 1, lines], gram_sent.at[at], gram_here.at[at], peer(*offset))
        owed.append((gram_recv.at[at, pl.ds(0, sizes[stage] - 1), lines], gram_sent.at[at]))

    def gram_end(stage):
        at = turn[stage]
        ref = gram_recv.at[at, pl.ds(0, sizes[stage] - 1), lines]
        wait_bytes(ref, gram_here.at[at])
        return gram_send[at, lines] + jnp.sum(gram_recv[at, pl.ds(0, sizes[stage] - 1), lines], axis=0)

    low_rad = (me[0] > 0).astype(F32)
    high_rad = (me[0] < n_rad - 1).astype(F32)
    low_lat = (me[1] > 0).astype(F32)
    high_lat = (me[1] < n_lat - 1).astype(F32)
    tile_masks = (1.0, 1.0, high_lat, jnp.where(sub < 4, high_lat, low_lat), low_lat)
    for block, rad_mask in ((0, low_rad), (1, 1.0), (2, high_rad)):
        sides = []
        for slot in range(3):
            right, left = packs[block, 0, slot], packs[block, 1, slot]
            tiles = []
            for spot in range(2 * RAD):
                a = pltpu.roll(right, (LON - GROUP * spot) % LON, 2) if spot else right
                b = pltpu.roll(left, LON - GROUP - GROUP * spot, 2) if spot < 7 else left
                tiles.append(jnp.where((lane < LON // 2)[None], a, b))
            sides.append(tiles)
        for layer in range(RAD):
            high, mid, low = (sides[s][2 * layer:2 * layer + 2] for s in (0, 1, 2))
            columns = (mid[0], mid[1], high[0], jnp.where((sub < 4)[None], high[1], low[0]), low[1])
            at = RAD * block + layer
            for t in range(5):
                mask = tile_masks[t] * rad_mask
                rows = pl.ds(8 * t, 8)
                main = raw[:, at, rows, :]
                ua[at, rows, pl.ds(0, LON)] = main[0] * mask
                ua[at, rows, pl.ds(LON, LON)] = columns[t][0] * mask
                ka[at, rows, pl.ds(0, LON)] = main[1] * (mask * radial_weight)
                ka[at, rows, pl.ds(LON, LON)] = columns[t][1] * (mask * radial_weight)

    def advance(src, dst, depth, pick, lo, hi, sides=None):
        rows = src.shape[1]

        def layer(r):
            if sides is not None and not RAD <= r < 2 * RAD:
                packed = sides[1 if r < RAD else 2]
                turn_by = (LON - 32 * (r % RAD)) % LON
                value = jnp.concatenate([src[r, :, pl.ds(0, LON)], pltpu.roll(packed, turn_by, 1) if turn_by else packed], axis=1)
            else:
                value = src[r]
            if lo is not None and r < RAD:
                value = value * lo
            if hi is not None and r >= 2 * RAD:
                value = value * hi
            return value

        before, here = layer(depth - 1), layer(depth)
        for r in range(depth, 3 * RAD - depth):
            after = layer(r + 1)
            lat = pltpu.roll(here, 1, 0) + pltpu.roll(here, rows - 1, 0)
            lon = pltpu.roll(here, 1, 1) + pltpu.roll(here, 2 * LON - 1, 1)
            dst(r, here + pick(r) * ((before + after) + 3.0 * lat + (5.0 * lon - 18.0 * here)))
            before, here = here, after

    def store(ref):
        def put(r, value):
            ref[r] = value
        return put

    def pick1(r):
        return ka[r]

    def pick2(r):
        return jnp.concatenate([ka[r, pl.ds(0, 24)], ka[r, pl.ds(32, 8)]], axis=0)

    wide_sub = lax.broadcasted_iota(jnp.int32, (8, 2 * LON), 0)

    def pick3(r):
        seam = jnp.where(wide_sub < 4, ka[r, pl.ds(16, 8)], ka[r, pl.ds(32, 8)])
        return jnp.concatenate([ka[r, pl.ds(0, 16)], seam], axis=0)

    def keep2(r, value):
        x2a[r, pl.ds(0, 24)] = value[0:24]
        x2a[r, pl.ds(24, 8)] = value[32:40]

    def keep3(r, value):
        x3a[r, pl.ds(0, 16)] = value[0:16]
        x3a[r, pl.ds(16, 8)] = jnp.where(wide_sub < 4, value[16:24], value[24:32])

    def exchange(ref, side, number):
        main = pl.ds(0, LON)
        for r in (1, -1):
            send(ref.at[own, :, main], ref.at[pl.ds(RAD * block_of(r), RAD), :, main], face_sent.at[number, 0],
                 face_here.at[number, 0], peer(r, 0, 0))
        group = (lax.broadcasted_iota(jnp.int32, side.shape[1:], 1) + GROUP) // 32
        packed = ref[RAD, :, pl.ds(LON, LON)]
        for l in range(1, RAD):
            packed = jnp.where(group == l, pltpu.roll(ref[RAD + l, :, pl.ds(LON, LON)], 32 * l, 1), packed)
        side[0] = packed
        for r in (1, -1):
            send(side.at[0], side.at[1 + block_of(r) // 2], face_sent.at[number, 1], face_here.at[number, 1], peer(r, 0, 0))
        owed.append((ref.at[pl.ds(0, 2 * RAD), :, main], face_sent.at[number, 0]))
        owed.append((side.at[pl.ds(1, 2)], face_sent.at[number, 1]))

    def exchanged(ref, side, number):
        wait_bytes(ref.at[pl.ds(0, 2 * RAD), :, pl.ds(0, LON)], face_here.at[number, 0])
        wait_bytes(side.at[pl.ds(1, 2)], face_here.at[number, 1])

    advance(ua, store(ub), 1, pick1, None, None)
    advance(ub, store(ua), 2, pick1, None, None)
    advance(ua, store(ub), 3, pick1, None, None)
    advance(ub, keep2, 4, pick1, None, None)
    exchange(x2a, side2, 0)
    pl.semaphore_wait(near_in, len(outer))
    for r in (-4, 4):
        pl.semaphore_signal(far_in, inc=1, device_id=peer(r, 0, 0), device_id_type=MESH)
    gram_start(1)
    exchanged(x2a, side2, 0)
    advance(x2a, store(x2b), 1, pick2, low_rad, high_rad, side2)
    advance(x2b, store(x2c), 2, pick2, None, None)
    advance(x2c, store(x2b), 3, pick2, None, None)
    advance(x2b, keep3, 4, pick2, None, None)
    exchange(x3a, side3, 1)
    pl.semaphore_wait(far_in, 2)
    gram_send[1, lines] = gram_end(1)
    gram_start(2)
    exchanged(x3a, side3, 1)
    advance(x3a, store(x3b), 1, pick3, low_rad, high_rad, side3)
    advance(x3b, store(x3c), 2, pick3, None, None)
    advance(x3c, store(x3b), 3, pick3, None, None)

    def finish(r, value):
        minus_smooth[r - RAD] = -value[0:LAT, 0:LON]

    advance(x3b, finish, 4, pick3, None, None)

    acc = [jnp.zeros((pairs, 8, LON), F32) for _ in range(2)]
    for spot in range(2 * RAD):
        rows = pl.ds(8 * (spot % 2), 8)
        field = -minus_smooth[spot // 2, rows, :][None]
        acc = [acc[h] + hist[h, :, spot // 2, rows, :] * field for h in range(2)]
    line = jnp.zeros((8, LON), F32)
    for h in range(2):
        sums = jnp.sum(acc[h], axis=2, keepdims=True)
        for i in range(pairs):
            line = jnp.where(lane == GROUP * h + i, sums[i], line)

    def hops(offset):
        return sum(min(d, n - d) for d, n in zip(offset, sizes))

    def add_up(buf, row, offsets, number):
        count = len(offsets)
        buf[pl.ds(count, 1)] = row
        for at, offset in enumerate(sorted(offsets, key=lambda c: -hops(c))):
            send(buf.at[pl.ds(count, 1)], buf.at[pl.ds(at, 1)], row_sent.at[number], row_here.at[number], peer(*offset))
        owed.append((buf.at[pl.ds(0, count)], row_sent.at[number]))

    def added(buf, offsets, number):
        count = len(offsets)
        wait_bytes(buf.at[pl.ds(0, count)], row_here.at[number])
        return jnp.sum(buf[pl.ds(0, count + 1)], axis=0, keepdims=True)

    in_plane = [(0, a, o) for a in range(n_lat) for o in range(n_lon)][1:]
    in_rad = [(r, 0, 0) for r in range(1, n_rad)]
    add_up(plane_row, jnp.sum(line, axis=0, keepdims=True), in_plane, 0)
    gram_send[2, lines] = gram_end(2)
    drain()
    gram_start(0)
    add_up(rad_row, added(plane_row, in_plane, 0), in_rad, 1)

    packed = gram_end(0)
    parts = [pltpu.roll(packed[i // 4:i // 4 + 1], LON - 32 * (i % 4), 1) if i % 4 else packed[i // 4:i // 4 + 1]
             for i in range(pairs)]
    gram = jnp.concatenate(parts + [jnp.zeros((16 - pairs, LON), F32)], axis=0)
    col = lax.broadcasted_iota(jnp.int32, (16, LON), 1)
    row = lax.broadcasted_iota(jnp.int32, (16, LON), 0)
    inside = row < pairs
    diagonal = (col == row) & inside
    d = jnp.sum(jnp.where(diagonal, gram, 0.0), axis=1, keepdims=True)
    inverse = 1.0 / jnp.where(inside[:, 0:1], d, 1.0)
    scaling = gram[pairs - 1:pairs, pairs - 1:pairs] / gram[pairs - 1:pairs, GROUP + pairs - 1:GROUP + pairs]
    upper = jnp.where((col > row) & (col < pairs), gram * inverse, 0.0)
    solve = jnp.where(diagonal, 1.0, 0.0)
    for k in range(pairs - 1, 0, -1):
        solve = solve - upper[:, k:k + 1] * solve[k:k + 1, :]
    inverse_row = jnp.sum(jnp.where(diagonal, inverse, 0.0), axis=0, keepdims=True)
    alpha = solve * inverse_row
    right = d * alpha
    for k in range(pairs):
        right = right + (scaling * gram[:, GROUP + k:GROUP + k + 1]) * alpha[k:k + 1, :]
    right = jnp.where((col == row + GROUP) & inside, -scaling, right)
    for k in range(pairs - 1):
        column = jnp.sum(jnp.where(col == row, upper[k:k + 1, :], 0.0), axis=1, keepdims=True)
        right = right - column * right[k:k + 1, :]
    of_s = right * inverse
    of_y = -scaling * alpha

    drain()
    b = added(rad_row, in_rad, 1)
    coef[0] = jnp.broadcast_to(jnp.sum(of_s * b, axis=1, keepdims=True), (16, LON))
    coef[1] = jnp.broadcast_to(jnp.sum(of_y * b, axis=1, keepdims=True), (16, LON))
    for spot in range(2 * RAD):
        rows = pl.ds(8 * (spot % 2), 8)
        value = -scaling * minus_smooth[spot // 2, rows, :]
        for i in range(pairs):
            value = value + coef[0, pl.ds(i, 1)] * hist[0, i, spot // 2, rows, :]
            value = value + coef[1, pl.ds(i, 1)] * hist[1, i, spot // 2, rows, :]
        minus_dir[spot // 2, rows, :] = value


def per_device(sizes, gradient, conductance, s_hist, y_hist):
    pairs = s_hist.shape[0]
    most = max(sizes)
    vmem, dma = pltpu.VMEM, pltpu.SemaphoreType.DMA
    inputs = [pltpu.with_memory_space_constraint(a, pltpu.HBM) for a in (gradient, conductance, s_hist, y_hist)]
    out = pl.pallas_call(
        functools.partial(kernel, sizes),
        out_shape=pltpu.VMEM((2,) + gradient.shape, F32),
        in_specs=[pl.BlockSpec(memory_space=pltpu.HBM)] * 4,
        out_specs=pl.BlockSpec(memory_space=vmem),
        scratch_shapes=[
            vmem((2, 3 * RAD, 40, LON), F32),
            vmem((2, pairs, RAD, LAT, LON), F32),
            vmem((2, 2, 8, LON), F32),
            vmem((3, 2, 3, 2, 8, LON), F32),
            vmem((3 * RAD, 40, 2 * LON), F32),
            vmem((3 * RAD, 40, 2 * LON), F32),
            vmem((3 * RAD, 40, 2 * LON), F32),
            vmem((3 * RAD, 32, 2 * LON), F32),
            vmem((3 * RAD, 32, 2 * LON), F32),
            vmem((3 * RAD, 32, 2 * LON), F32),
            vmem((3 * RAD, 24, 2 * LON), F32),
            vmem((3 * RAD, 24, 2 * LON), F32),
            vmem((3 * RAD, 24, 2 * LON), F32),
            vmem((3, 32, LON), F32),
            vmem((3, 24, LON), F32),
            vmem((3, 8, LON), F32),
            vmem((3, most - 1, 8, LON), F32),
            vmem((sizes[1] * sizes[2], LON), F32),
            vmem((sizes[0], LON), F32),
            vmem((2, 16, LON), F32),
            dma((4,)),
            dma((4,)),
            dma((4,)),
            dma((2, 2)),
            dma((2, 2)),
            dma((3,)),
            dma((3,)),
            dma((2,)),
            dma((2,)),
            pltpu.SemaphoreType.REGULAR,
            pltpu.SemaphoreType.REGULAR,
        ],
        compiler_params=pltpu.CompilerParams(collective_id=0, has_side_effects=True, vmem_limit_bytes=24 * 2**20),
        cost_estimate=pl.CostEstimate(flops=20_000_000, bytes_accessed=800_000, transcendentals=0),
        name="filter_and_direction",
    )(*inputs)
    return -out[0], -out[1]


def solution(mesh):
    sizes = tuple(mesh.shape[a] for a in AXES)
    field, history = P(*AXES), P(None, *AXES)
    return jax.shard_map(
        functools.partial(per_device, sizes),
        mesh=mesh,
        in_specs=(field, field, history, history),
        out_specs=(field, field),
        check_vma=False,
    )
```

```python
import functools

import jax
import jax.numpy as jnp
from jax import lax
from jax.experimental import pallas as pl
from jax.experimental.pallas import tpu as pltpu
from jax.sharding import PartitionSpec as P

STEPS = 12
AXES = ("rad", "lat", "lon")
MESH = pl.DeviceIdType.MESH

RAD, LAT, LON = 4, 16, 128
WIDE = 12
GROUP = 16
radial_weight = 0.05
latitude_weight = 0.15
longitude_weight = 0.25
F32 = jnp.float32


def ordered(n):
    return sorted(range(1, n), key=lambda d: -min(d, n - d))


def kernel(sizes, g_hbm, k_hbm, s_hbm, y_hbm, out_ref, raw, hist, edges, packs, ua, ka, ub, x2a, x2b, x2c, x3a,
           x3b, x3c, side2, side3, va, vb, near_hist, gram_send, gram_recv, plane_row, rad_row, coef, load_sem, halo_sent, halo_here, face_sent, face_here,
           gram_sent, gram_here, row_sent, row_here, hist_sent, hist_here, near_in, far_in):
    n_rad, n_lat, n_lon = sizes
    pairs = s_hbm.shape[0]
    minus_smooth, minus_dir = out_ref.at[0], out_ref.at[1]
    me = tuple(lax.axis_index(a) for a in AXES)

    def peer(*offset):
        return tuple(lax.rem(m + (o % n), n) if o % n else m for m, o, n in zip(me, offset, sizes))

    owed = []

    def send(src, dst, ssem, rsem, target):
        pltpu.make_async_remote_copy(src_ref=src, dst_ref=dst, send_sem=ssem, recv_sem=rsem, device_id=target,
                                     device_id_type=MESH).start()

    def wait_bytes(ref, sem):
        pltpu.make_async_copy(ref, ref, sem).wait()

    load_g = pltpu.make_async_copy(g_hbm, raw.at[0, pl.ds(RAD, RAD), pl.ds(0, LAT)], load_sem.at[0])
    load_k = pltpu.make_async_copy(k_hbm, raw.at[1, pl.ds(RAD, RAD), pl.ds(0, LAT)], load_sem.at[1])
    load_s = pltpu.make_async_copy(s_hbm, hist.at[0], load_sem.at[2])
    load_y = pltpu.make_async_copy(y_hbm, hist.at[1], load_sem.at[3])
    for copy in (load_g, load_k, load_s, load_y):
        copy.start()

    near = (0, -1, 1)
    cube = [(r, a, o) for r in near for a in near for o in near][1:]
    cube.sort(key=lambda c: -sum(map(abs, c)))
    partners = cube + [(-2, 0, 0), (2, 0, 0)] + [(0, a, 0) for a in range(2, n_lat - 1)]
    barrier = pltpu.get_barrier_semaphore()
    for offset in partners:
        pl.semaphore_signal(barrier, inc=1, device_id=peer(*offset), device_id_type=MESH)

    lane = lax.broadcasted_iota(jnp.int32, (8, LON), 1)
    sub = lax.broadcasted_iota(jnp.int32, (8, LON), 0)

    load_g.wait()
    load_k.wait()
    to_right = jnp.zeros((2, 8, LON), F32)
    to_left = jnp.zeros((2, 8, LON), F32)
    for spot in range(2 * RAD):
        tile = raw[:, RAD + spot // 2, pl.ds(8 * (spot % 2), 8), :]
        here = (lane // GROUP == spot)[None]
        to_right = jnp.where(here, pltpu.roll(tile, (GROUP * spot + GROUP) % LON, 2), to_right)
        to_left = jnp.where(here, pltpu.roll(tile, GROUP * spot, 2) if spot else tile, to_left)
    edges[0] = to_left
    edges[1] = to_right

    pl.semaphore_wait(barrier, len(partners))

    own = pl.ds(RAD, RAD)

    def block_of(r):
        return 1 - r

    rows_of = {-1: (0, WIDE, LAT), 0: (0, LAT, 0), 1: (LAT - WIDE, WIDE, LAT + WIDE)}

    def halo(r, a, o):
        at = block_of(r)
        if o:
            side = (o + 1) // 2
            send(edges.at[side], packs.at[at, side, 1 + a], halo_sent.at[3], halo_here.at[3], peer(r, a, o))
        else:
            first, count, to = rows_of[a]
            send(raw.at[:, own, pl.ds(first, count)], raw.at[:, pl.ds(RAD * at, RAD), pl.ds(to, count)], halo_sent.at[at],
                 halo_here.at[at], peer(r, a, o))

    for offset in cube:
        halo(*offset)
    halos = ((raw.at[:, pl.ds(0, RAD)], 0), (raw.at[:, own, pl.ds(LAT, 2 * WIDE)], 1), (raw.at[:, pl.ds(2 * RAD, RAD)], 2),
             (packs, 3))
    owed += [(ref, halo_sent.at[number]) for ref, number in halos]

    load_s.wait()
    load_y.wait()
    odd = lax.rem(me[0], 2)

    def along(step):
        return (lax.rem(me[0] + step + n_rad, n_rad), me[1], me[2])

    send(hist, near_hist.at[odd], hist_sent.at[0], hist_here.at[0], along(1 - 2 * odd))
    send(hist.at[0], near_hist.at[1 - odd, 0], hist_sent.at[1], hist_here.at[1], along(2 * odd - 1))
    owed += [(near_hist.at[0], hist_sent.at[0]), (near_hist.at[1], hist_sent.at[1])]

    def pass_on():
        wait_bytes(near_hist.at[0], hist_here.at[0])
        send(near_hist.at[1 - odd, 1], near_hist.at[odd, 1], hist_sent.at[1], hist_here.at[1], along(2 - 4 * odd))

    total = [jnp.zeros((8, LON), F32) for _ in range(-(-pairs // 4))]
    for j in range(pairs):
        if j == pairs // 2:
            pass_on()
        acc_s = jnp.zeros((pairs, 8, LON), F32)
        acc_y = jnp.zeros((pairs, 8, LON), F32)
        for spot in range(2 * RAD):
            rows = pl.ds(8 * (spot % 2), 8)
            one = hist[1, j, spot // 2, rows, :][None]
            acc_s += hist[0, :, spot // 2, rows, :] * one
            acc_y += hist[1, :, spot // 2, rows, :] * one
        sum_s = jnp.sum(acc_s, axis=2, keepdims=True)
        sum_y = jnp.sum(acc_y, axis=2, keepdims=True)
        for i in range(pairs):
            at = 32 * (i % 4) + j
            total[i // 4] = jnp.where(lane == at, sum_s[i], jnp.where(lane == at + GROUP, sum_y[i], total[i // 4]))
    for line, value in enumerate(total):
        gram_send[0, pl.ds(line, 1)] = jnp.sum(value, axis=0, keepdims=True)
    lines = pl.ds(0, len(total))

    turn = {1: 0, 2: 1, 0: 2}

    def gram_start(stage):
        at = turn[stage]
        for d in ordered(sizes[stage]):
            offset = [0, 0, 0]
            offset[stage] = d
            send(gram_send.at[at, lines], gram_recv.at[at, d - 1, lines], gram_sent.at[at], gram_here.at[at], peer(*offset))
        owed.append((gram_recv.at[at, pl.ds(0, sizes[stage] - 1), lines], gram_sent.at[at]))

    def gram_end(stage):
        at = turn[stage]
        ref = gram_recv.at[at, pl.ds(0, sizes[stage] - 1), lines]
        wait_bytes(ref, gram_here.at[at])
        return gram_send[at, lines] + jnp.sum(gram_recv[at, pl.ds(0, sizes[stage] - 1), lines], axis=0)

    gram_start(1)

    for ref, number in halos:
        wait_bytes(ref, halo_here.at[number])

    signs = (0, -2, 2)
    outer = [(0, a, o) for a in signs for o in signs][1:] + [(-2, 0, 0), (2, 0, 0)]
    for offset in outer:
        pl.semaphore_signal(near_in, inc=1, device_id=peer(*offset), device_id_type=MESH)

    low_rad = (me[0] > 0).astype(F32)
    high_rad = (me[0] < n_rad - 1).astype(F32)
    low_lat = (me[1] > 0).astype(F32)
    high_lat = (me[1] < n_lat - 1).astype(F32)
    tile_masks = (1.0, 1.0, high_lat, jnp.where(sub < 4, high_lat, low_lat), low_lat)
    for block, rad_mask in ((0, low_rad), (1, 1.0), (2, high_rad)):
        sides = []
        for slot in range(3):
            right, left = packs[block, 0, slot], packs[block, 1, slot]
            tiles = []
            for spot in range(2 * RAD):
                a = pltpu.roll(right, (LON - GROUP * spot) % LON, 2) if spot else right
                b = pltpu.roll(left, LON - GROUP - GROUP * spot, 2) if spot < 7 else left
                tiles.append(jnp.where((lane < LON // 2)[None], a, b))
            sides.append(tiles)
        for layer in range(RAD):
            high, mid, low = (sides[s][2 * layer:2 * layer + 2] for s in (0, 1, 2))
            columns = (mid[0], mid[1], high[0], jnp.where((sub < 4)[None], high[1], low[0]), low[1])
            at = RAD * block + layer
            for t in range(5):
                mask = tile_masks[t] * rad_mask
                rows = pl.ds(8 * t, 8)
                main = raw[:, at, rows, :]
                ua[at, rows, pl.ds(0, LON)] = main[0] * mask
                ua[at, rows, pl.ds(LON, LON)] = columns[t][0] * mask
                ka[at, rows, pl.ds(0, LON)] = main[1] * (mask * radial_weight)
                ka[at, rows, pl.ds(LON, LON)] = columns[t][1] * (mask * radial_weight)

    def advance(src, dst, depth, pick, lo, hi, sides=None):
        rows = src.shape[1]

        def layer(r):
            if sides is not None and not RAD <= r < 2 * RAD:
                packed = sides[1 if r < RAD else 2]
                turn_by = (LON - 32 * (r % RAD)) % LON
                value = jnp.concatenate([src[r, :, pl.ds(0, LON)], pltpu.roll(packed, turn_by, 1) if turn_by else packed], axis=1)
            else:
                value = src[r]
            if lo is not None and r < RAD:
                value = value * lo
            if hi is not None and r >= 2 * RAD:
                value = value * hi
            return value

        before, here = layer(depth - 1), layer(depth)
        for r in range(depth, 3 * RAD - depth):
            after = layer(r + 1)
            lat = pltpu.roll(here, 1, 0) + pltpu.roll(here, rows - 1, 0)
            lon = pltpu.roll(here, 1, 1) + pltpu.roll(here, 2 * LON - 1, 1)
            dst(r, here + pick(r) * ((before + after) + 3.0 * lat + (5.0 * lon - 18.0 * here)))
            before, here = here, after

    def store(ref):
        def put(r, value):
            ref[r] = value
        return put

    def pick1(r):
        return ka[r]

    def pick2(r):
        return jnp.concatenate([ka[r, pl.ds(0, 24)], ka[r, pl.ds(32, 8)]], axis=0)

    wide_sub = lax.broadcasted_iota(jnp.int32, (8, 2 * LON), 0)

    def pick3(r):
        seam = jnp.where(wide_sub < 4, ka[r, pl.ds(16, 8)], ka[r, pl.ds(32, 8)])
        return jnp.concatenate([ka[r, pl.ds(0, 16)], seam], axis=0)

    def keep2(r, value):
        x2a[r, pl.ds(0, 24)] = value[0:24]
        x2a[r, pl.ds(24, 8)] = value[32:40]

    def keep3(r, value):
        x3a[r, pl.ds(0, 16)] = value[0:16]
        x3a[r, pl.ds(16, 8)] = jnp.where(wide_sub < 4, value[16:24], value[24:32])

    def exchange(ref, side, number):
        main = pl.ds(0, LON)
        for r in (1, -1):
            send(ref.at[own, :, main], ref.at[pl.ds(RAD * block_of(r), RAD), :, main], face_sent.at[number, 0],
                 face_here.at[number, 0], peer(r, 0, 0))
        group = (lax.broadcasted_iota(jnp.int32, side.shape[1:], 1) + GROUP) // 32
        packed = ref[RAD, :, pl.ds(LON, LON)]
        for l in range(1, RAD):
            packed = jnp.where(group == l, pltpu.roll(ref[RAD + l, :, pl.ds(LON, LON)], 32 * l, 1), packed)
        side[0] = packed
        for r in (1, -1):
            send(side.at[0], side.at[1 + block_of(r) // 2], face_sent.at[number, 1], face_here.at[number, 1], peer(r, 0, 0))
        owed.append((ref.at[pl.ds(0, 2 * RAD), :, main], face_sent.at[number, 0]))
        owed.append((side.at[pl.ds(1, 2)], face_sent.at[number, 1]))

    def exchanged(ref, side, number):
        wait_bytes(ref.at[pl.ds(0, 2 * RAD), :, pl.ds(0, LON)], face_here.at[number, 0])
        wait_bytes(side.at[pl.ds(1, 2)], face_here.at[number, 1])

    advance(ua, store(ub), 1, pick1, None, None)
    advance(ub, store(ua), 2, pick1, None, None)
    advance(ua, store(ub), 3, pick1, None, None)
    advance(ub, keep2, 4, pick1, None, None)
    exchange(x2a, side2, 0)
    pl.semaphore_wait(near_in, len(outer))
    for r in (-4, 4):
        pl.semaphore_signal(far_in, inc=1, device_id=peer(r, 0, 0), device_id_type=MESH)
    gram_send[1, lines] = gram_end(1)
    gram_start(2)
    exchanged(x2a, side2, 0)
    advance(x2a, store(x2b), 1, pick2, low_rad, high_rad, side2)
    advance(x2b, store(x2c), 2, pick2, None, None)
    advance(x2c, store(x2b), 3, pick2, None, None)
    advance(x2b, keep3, 4, pick2, None, None)
    exchange(x3a, side3, 1)

    def spread(src, dst, step):
        first, last = RAD - step, 2 * RAD - 1 + step

        def layer(r):
            return src[r] if first < r < last else None

        def plus(a, b):
            return b if a is None else a if b is None else a + b

        for r in range(first, last + 1):
            here, around = layer(r), plus(layer(r - 1), layer(r + 1))
            if here is None:
                dst[r] = pick3(r) * around
                continue
            lat = pltpu.roll(here, 1, 0) + pltpu.roll(here, here.shape[0] - 1, 0)
            lon = pltpu.roll(here, 1, 1) + pltpu.roll(here, 2 * LON - 1, 1)
            dst[r] = here + pick3(r) * (around + 3.0 * lat + (5.0 * lon - 18.0 * here))

    spread(x3a, va, 1)
    spread(va, vb, 2)
    spread(vb, va, 3)
    spread(va, vb, 4)

    wait_bytes(near_hist.at[1], hist_here.at[1])
    acc = [jnp.zeros((pairs, 8, LON), F32) for _ in range(2)]
    for r in range(3 * RAD):
        for half in range(LAT // 8):
            rows = pl.ds(8 * half, 8)
            field = vb[r, rows, pl.ds(0, LON)][None]
            for h in range(2):
                if RAD <= r < 2 * RAD:
                    values = hist[h, :, r - RAD, rows, :]
                else:
                    values = near_hist[r // (2 * RAD), h, :, r % RAD, rows, :]
                acc[h] = acc[h] + values * field
    line = jnp.zeros((8, LON), F32)
    for h in range(2):
        sums = jnp.sum(acc[h], axis=2, keepdims=True)
        for i in range(pairs):
            line = jnp.where(lane == GROUP * h + i, sums[i], line)

    def hops(offset):
        return sum(min(d, n - d) for d, n in zip(offset, sizes))

    def add_up(buf, row, offsets, number):
        count = len(offsets)
        buf[pl.ds(count, 1)] = row
        for at, offset in enumerate(sorted(offsets, key=lambda c: -hops(c))):
            send(buf.at[pl.ds(count, 1)], buf.at[pl.ds(at, 1)], row_sent.at[number], row_here.at[number], peer(*offset))
        owed.append((buf.at[pl.ds(0, count)], row_sent.at[number]))

    def added(buf, offsets, number):
        count = len(offsets)
        wait_bytes(buf.at[pl.ds(0, count)], row_here.at[number])
        return jnp.sum(buf[pl.ds(0, count + 1)], axis=0, keepdims=True)

    in_plane = [(0, a, o) for a in range(n_lat) for o in range(n_lon)][1:]
    in_rad = [(r, 0, 0) for r in range(1, n_rad)]
    add_up(plane_row, jnp.sum(line, axis=0, keepdims=True), in_plane, 0)
    pl.semaphore_wait(far_in, 2)
    gram_send[2, lines] = gram_end(2)
    gram_start(0)
    exchanged(x3a, side3, 1)
    advance(x3a, store(x3b), 1, pick3, low_rad, high_rad, side3)
    advance(x3b, store(x3c), 2, pick3, None, None)
    advance(x3c, store(x3b), 3, pick3, None, None)

    def finish(r, value):
        minus_smooth[r - RAD] = -value[0:LAT, 0:LON]

    advance(x3b, finish, 4, pick3, None, None)

    add_up(rad_row, added(plane_row, in_plane, 0), in_rad, 1)

    packed = gram_end(0)
    parts = [pltpu.roll(packed[i // 4:i // 4 + 1], LON - 32 * (i % 4), 1) if i % 4 else packed[i // 4:i // 4 + 1]
             for i in range(pairs)]
    gram = jnp.concatenate(parts + [jnp.zeros((16 - pairs, LON), F32)], axis=0)
    col = lax.broadcasted_iota(jnp.int32, (16, LON), 1)
    row = lax.broadcasted_iota(jnp.int32, (16, LON), 0)
    inside = row < pairs
    diagonal = (col == row) & inside
    d = jnp.sum(jnp.where(diagonal, gram, 0.0), axis=1, keepdims=True)
    inverse = 1.0 / jnp.where(inside[:, 0:1], d, 1.0)
    scaling = gram[pairs - 1:pairs, pairs - 1:pairs] / gram[pairs - 1:pairs, GROUP + pairs - 1:GROUP + pairs]
    upper = jnp.where((col > row) & (col < pairs), gram * inverse, 0.0)
    solve = jnp.where(diagonal, 1.0, 0.0)
    for k in range(pairs - 1, 0, -1):
        solve = solve - upper[:, k:k + 1] * solve[k:k + 1, :]
    inverse_row = jnp.sum(jnp.where(diagonal, inverse, 0.0), axis=0, keepdims=True)
    alpha = solve * inverse_row
    right = d * alpha
    for k in range(pairs):
        right = right + (scaling * gram[:, GROUP + k:GROUP + k + 1]) * alpha[k:k + 1, :]
    right = jnp.where((col == row + GROUP) & inside, -scaling, right)
    for k in range(pairs - 1):
        column = jnp.sum(jnp.where(col == row, upper[k:k + 1, :], 0.0), axis=1, keepdims=True)
        right = right - column * right[k:k + 1, :]
    of_s = right * inverse
    of_y = -scaling * alpha

    b = added(rad_row, in_rad, 1)
    coef[0] = jnp.broadcast_to(jnp.sum(of_s * b, axis=1, keepdims=True), (16, LON))
    coef[1] = jnp.broadcast_to(jnp.sum(of_y * b, axis=1, keepdims=True), (16, LON))
    for spot in range(2 * RAD):
        rows = pl.ds(8 * (spot % 2), 8)
        value = -scaling * minus_smooth[spot // 2, rows, :]
        for i in range(pairs):
            value = value + coef[0, pl.ds(i, 1)] * hist[0, i, spot // 2, rows, :]
            value = value + coef[1, pl.ds(i, 1)] * hist[1, i, spot // 2, rows, :]
        minus_dir[spot // 2, rows, :] = value

    for ref, sem in owed:
        wait_bytes(ref, sem)


def per_device(sizes, gradient, conductance, s_hist, y_hist):
    pairs = s_hist.shape[0]
    most = max(sizes)
    vmem, dma = pltpu.VMEM, pltpu.SemaphoreType.DMA
    inputs = [pltpu.with_memory_space_constraint(a, pltpu.HBM) for a in (gradient, conductance, s_hist, y_hist)]
    out = pl.pallas_call(
        functools.partial(kernel, sizes),
        out_shape=pltpu.VMEM((2,) + gradient.shape, F32),
        in_specs=[pl.BlockSpec(memory_space=pltpu.HBM)] * 4,
        out_specs=pl.BlockSpec(memory_space=vmem),
        scratch_shapes=[
            vmem((2, 3 * RAD, 40, LON), F32),
            vmem((2, pairs, RAD, LAT, LON), F32),
            vmem((2, 2, 8, LON), F32),
            vmem((3, 2, 3, 2, 8, LON), F32),
            vmem((3 * RAD, 40, 2 * LON), F32),
            vmem((3 * RAD, 40, 2 * LON), F32),
            vmem((3 * RAD, 40, 2 * LON), F32),
            vmem((3 * RAD, 32, 2 * LON), F32),
            vmem((3 * RAD, 32, 2 * LON), F32),
            vmem((3 * RAD, 32, 2 * LON), F32),
            vmem((3 * RAD, 24, 2 * LON), F32),
            vmem((3 * RAD, 24, 2 * LON), F32),
            vmem((3 * RAD, 24, 2 * LON), F32),
            vmem((3, 32, LON), F32),
            vmem((3, 24, LON), F32),
            vmem((3 * RAD, 24, 2 * LON), F32),
            vmem((3 * RAD, 24, 2 * LON), F32),
            vmem((2, 2, pairs, RAD, LAT, LON), F32),
            vmem((3, 8, LON), F32),
            vmem((3, most - 1, 8, LON), F32),
            vmem((sizes[1] * sizes[2], LON), F32),
            vmem((sizes[0], LON), F32),
            vmem((2, 16, LON), F32),
            dma((4,)),
            dma((4,)),
            dma((4,)),
            dma((2, 2)),
            dma((2, 2)),
            dma((3,)),
            dma((3,)),
            dma((2,)),
            dma((2,)),
            dma((2,)),
            dma((2,)),
            pltpu.SemaphoreType.REGULAR,
            pltpu.SemaphoreType.REGULAR,
        ],
        compiler_params=pltpu.CompilerParams(collective_id=0, has_side_effects=True, vmem_limit_bytes=24 * 2**20),
        cost_estimate=pl.CostEstimate(flops=20_000_000, bytes_accessed=800_000, transcendentals=0),
        name="filter_and_direction",
    )(*inputs)
    return -out[0], -out[1]


def solution(mesh):
    sizes = tuple(mesh.shape[a] for a in AXES)
    field, history = P(*AXES), P(None, *AXES)
    return jax.shard_map(
        functools.partial(per_device, sizes),
        mesh=mesh,
        in_specs=(field, field, history, history),
        out_specs=(field, field),
        check_vma=False,
    )
```
